512 devices in a mesh: lon: 16 (over y_lo, x), lat: 8 (over z), mem: 4 (over y_hi, core).
Axes of the slice: x: 4, y: 8 (y_hi: 2, y_lo: 4; y = y_hi * 4 + y_lo), z: 8, core: 2. Of those that a mesh axis runs over, the one named last changes fastest.
Arguments:
- anomalies: bfloat16 [80, 128, 2048], P('mem', 'lat', 'lon'), may hold values from -6 to 6
- vector: bfloat16 [128, 2048], P('lat', 'lon'), may hold values from -6 to 6
- cotangent: bfloat16 [128, 2048], P('lat', 'lon'), may hold values from -6 to 6
- taper: bfloat16 [289, 128, 2048], P(None, ('lat', 'mem'), 'lon'), may hold values from 0 to 1
Outputs:
- grad_taper: float32 [289, 128, 2048], P(None, ('lat', 'mem'), 'lon')
- grad_anomalies: float32 [80, 128, 2048], P('mem', 'lat', 'lon')
The draws below stay inside these ranges and needn't reach their ends.
All inputs are finite; a program needn't handle non-finite values.
Results may differ from the reference program's by a relative error of at most 0.00035.
Values may be sent and summed in bfloat16 or wider, within the bound.
No kernel may reach another device: no remote copies, remote signals or barrier semaphores. Data moves between devices by JAX's collectives and lax.ppermute only.
A program may use at most 64 MiB of HBM per device.

```python
import jax
import jax.numpy as jnp
from jax import lax

SPAN = 17
TAPS = 289
MEMBERS = 80
NLAT = 128
NLON = 2048


def levels(key, shape, split, low, high):
    gain = 1.0
    for dim, shards_of in split:
        steps = jax.random.uniform(jax.random.fold_in(jax.random.fold_in(key, 6), dim), (shards_of,), jnp.float32, low / len(split), high / len(split))
        gain = gain * jnp.repeat(jnp.exp(steps), shape[dim] // shards_of).reshape((-1,) + (1,) * (len(shape) - 1 - dim))
    return gain


def gaussian(own_key, extent, width, limit, split=(), kind=jnp.bfloat16):
    result = jax.random.normal(own_key, extent, jnp.float32) * width
    if len(split) > 0:
        result = levels(own_key, extent, split, -0.22, 0.18) * result
    return jnp.clip(result, min=-limit, max=limit).astype(kind)


def setup_inputs(seed: int = 0) -> dict:
    key_of = jax.random.split(jax.random.key(seed), 5)
    anomalies = gaussian(key_of[0], (MEMBERS, NLAT, NLON), 1.0, 6.0, ((0, 4), (1, 8), (2, 16)))
    vector = gaussian(key_of[1], (NLAT, NLON), 1.0, 6.0, ((0, 8), (1, 16)))
    cotangent = gaussian(key_of[2], (NLAT, NLON), 1.0, 6.0, ((0, 8), (1, 16)))
    taper = jnp.clip(1.0 * jax.random.uniform(key_of[3], (TAPS, NLAT, NLON), jnp.float32) ** levels(key_of[3], (TAPS, NLAT, NLON), ((1, 32), (2, 16)), -0.2, 0.2), 0.0, 1.0).astype(jnp.bfloat16)
    return dict(anomalies=anomalies, vector=vector, cotangent=cotangent, taper=taper)


def pad_grid(field, rim):
    wrapped = jnp.concatenate([field[..., -rim:], field, field[..., :rim]], axis=-1)
    widths = [(0, 0)] * (field.ndim - 2) + [(rim, rim), (0, 0)]
    return jnp.pad(wrapped, widths)


def reference(anomalies, vector, cotangent, taper):
    rim = SPAN // 2
    states = anomalies.astype(jnp.float32)
    field = vector.astype(jnp.float32)
    grad_in = cotangent.astype(jnp.float32)
    padded_x = pad_grid(states, rim)
    padded_v = pad_grid(field, rim)
    zero = jnp.int32(0)

    def step(carry, tap):
        first, second = carry
        row_off = (tap // SPAN).astype(jnp.int32)
        col_off = (tap % SPAN).astype(jnp.int32)
        moved_x = lax.dynamic_slice(padded_x, (zero, row_off, col_off), (MEMBERS, NLAT, NLON))
        moved_v = lax.dynamic_slice(padded_v, (row_off, col_off), (NLAT, NLON))
        cov = jnp.sum(states * moved_x, axis=0) / (MEMBERS - 1)
        weight = lax.dynamic_index_in_dim(taper, tap, 0, keepdims=False).astype(jnp.float32)
        scaled = grad_in * weight
        first = first + (scaled * moved_v)[None] * moved_x
        pushed = pad_grid(scaled[None] * states, rim)
        back = lax.dynamic_slice(pushed, (zero, 2 * rim - row_off, 2 * rim - col_off), (MEMBERS, NLAT, NLON))
        second = second + back
        return (first, second), grad_in * cov * moved_v

    init = (jnp.zeros((MEMBERS, NLAT, NLON), jnp.float32), jnp.zeros((MEMBERS, NLAT, NLON), jnp.float32))
    (first, second), grad_taper = lax.scan(step, init, jnp.arange(TAPS, dtype=jnp.int32))
    grad_anomalies = (first + field[None] * second) / (MEMBERS - 1)
    return grad_taper, grad_anomalies
```

```python
import functools

import jax
import jax.numpy as jnp
from jax import lax
from jax.experimental import pallas as pl
from jax.experimental.pallas import tpu as pltpu
from jax.sharding import PartitionSpec as P

SPAN = 17
RIM = 8
TAPS = SPAN * SPAN
ROWS = 4
CLAT = 16
LON = 128
WIN = ROWS + 2 * RIM
RING = CLAT + RIM
GROUP = 20
MEMBERS = 80
DEPTH = 88
PART = GROUP * CLAT + 2 * GROUP
EDGES = 64
TAPE = 24
HALO = 3 * LON
LATROWS = MEMBERS * RIM + MEMBERS + RIM + 8
F32 = jnp.float32
BF16 = jnp.bfloat16
SMEM = pltpu.SMEM
VMEM = pltpu.VMEM


def lanes(shape):
    return lax.broadcasted_iota(jnp.int32, shape, len(shape) - 1)


def rows_of(shape):
    return lax.broadcasted_iota(jnp.int32, shape, len(shape) - 2)


def call(kernel, out_shape, scratch, *args):
    specs = [pl.BlockSpec(memory_space=SMEM)] + [pl.BlockSpec(memory_space=VMEM)] * (len(args) - 1)
    return pl.pallas_call(
        kernel,
        out_shape=out_shape,
        in_specs=specs,
        out_specs=jax.tree.map(lambda _: pl.BlockSpec(memory_space=VMEM), out_shape),
        scratch_shapes=scratch,
        compiler_params=pltpu.CompilerParams(vmem_limit_bytes=48 * 2**20),
    )(*args)


def shape(*dims, dtype=F32):
    return jax.ShapeDtypeStruct(dims, dtype)


def unpack_taper(taper_ref, wide):
    for tap in range(TAPS):
        wide[tap * ROWS : tap * ROWS + ROWS] = taper_ref[tap].astype(F32)


def edges_kernel(mem_ref, x_ref, v_ref, c_ref, taper_ref, left_ref, right_ref, wide, cells):
    unpack_taper(taper_ref, wide)
    cells[0 : GROUP * CLAT] = x_ref[...].astype(F32).reshape(GROUP * CLAT, LON)
    cells[GROUP * CLAT : (GROUP + 1) * CLAT] = v_ref[...].astype(F32)
    cells[(GROUP + 1) * CLAT : (GROUP + 2) * CLAT] = c_ref[...].astype(F32)
    cells[(GROUP + 2) * CLAT :] = jnp.zeros((2 * CLAT, LON), F32)
    lane = lanes((TAPE, LON))
    left = jnp.zeros((TAPE, LON), F32)
    right = jnp.zeros((TAPE, LON), F32)
    for lat in range(CLAT):
        part = cells[pl.ds(lat, TAPE, stride=CLAT), :]
        mine = lane // RIM == lat
        left = jnp.where(mine, pltpu.roll(part, RIM * lat, 1), left)
        right = jnp.where(mine, pltpu.roll(part, (RIM * lat + RIM) % LON, 1), right)
    left_ref[0:TAPE] = left.astype(BF16)
    right_ref[0:TAPE] = right.astype(BF16)
    lane = lanes((8, LON))
    row = rows_of((8, LON))
    for block in range(5):
        left = jnp.zeros((8, LON), F32)
        right = jnp.zeros((8, LON), F32)
        for sub in range(4):
            a = block * 4 + sub
            if a >= SPAN:
                continue
            for i in range(ROWS):
                to = sub * 32 + i * RIM
                mine = lane // RIM == to // RIM
                part = wide[pl.ds(a * SPAN * ROWS + i, 8, stride=ROWS), :]
                left = jnp.where(mine, pltpu.roll(part, to, 1), left)
                part = wide[pl.ds((a * SPAN + 9) * ROWS + i, 8, stride=ROWS), :]
                right = jnp.where(mine, pltpu.roll(part, (to + RIM) % LON, 1), right)
        for bit in (1, 2, 4):
            moved = pltpu.roll(left, bit, 0)
            moved = jnp.where(row >= bit, moved, 0.0)
            left = jnp.where((lane & bit) != 0, moved, left)
            moved = pltpu.roll(right, 8 - bit, 0)
            moved = jnp.where(row < 8 - bit, moved, 0.0)
            right = jnp.where(((7 - lane) & bit) != 0, moved, right)
        at = TAPE + 8 * block
        left_ref[at : at + 8] = left.astype(BF16)
        right_ref[at : at + 8] = right.astype(BF16)


def edge_messages(mem, anomalies, vector, cotangent, taper):
    return call(
        edges_kernel,
        (shape(EDGES, LON, dtype=BF16),) * 2,
        [
            VMEM((TAPS * ROWS + 4, LON), F32),
            VMEM(((GROUP + 4) * CLAT, LON), F32),
        ],
        mem,
        anomalies,
        vector,
        cotangent,
        taper,
    )


def ring_row(mem, j):
    lat = ROWS * mem - RIM + j
    return jnp.where(lat < 0, lat + RING, lat)


def halo_row(side, ring):
    inside = side * LON + RIM * ring
    outside = 2 * LON + side * (LON // 2) + RIM * (ring - CLAT)
    return pl.multiple_of(jnp.where(ring < CLAT, inside, outside), 8)


def bands_kernel(mem_ref, taper_ref, band_ref, rim_ref, wide, narrow):
    mem = mem_ref[0]
    unpack_taper(taper_ref, wide)
    narrow[...] = jnp.zeros(narrow.shape, F32)
    for i in range(ROWS):
        for j in range(WIN):
            if j < i or j > i + SPAN - 1:
                band_ref[j * LON : (j + 1) * LON, i * LON : (i + 1) * LON] = jnp.zeros(
                    (LON, LON), BF16
                )
    lane = lanes((24, LON))
    row = rows_of((24, LON))
    group = lanes((8, LON)) // 8
    zero = jnp.zeros((8, LON), F32)

    @pl.loop(0, SPAN)
    def _(a):
        for i in range(ROWS):
            taps = wide[pl.ds(a * SPAN * ROWS + i, 24, stride=ROWS), :]
            taps = jnp.where(row < SPAN, taps, 0.0)
            for bit in (1, 2, 4):
                taps = jnp.where((lane & bit) != 0, pltpu.roll(taps, bit, 0), taps)
            low, mid, high = taps[0:8], taps[8:16], taps[16:24]
            parts = []
            for block in range(CLAT):
                part = jnp.where(group == block, mid, zero)
                if block < 15:
                    part = jnp.where(group == block + 1, low, part)
                if block > 0:
                    part = jnp.where(group == block - 1, high, part)
                parts.append(part)
            band_ref[pl.ds(pl.multiple_of((a + i) * LON, LON), LON), i * LON : (i + 1) * LON] = (
                jnp.concatenate(parts, 0).astype(BF16)
            )
            ring = ring_row(mem, a + i)
            narrow[pl.ds(halo_row(0, ring), 8), i * LON : (i + 1) * LON] = jnp.where(
                group == 15, high, zero
            )
            narrow[pl.ds(halo_row(1, ring), 8), i * LON : (i + 1) * LON] = jnp.where(
                group == 0, low, zero
            )

    rim_ref[...] = narrow[...].astype(BF16)


def bands(mem, taper):
    return call(
        bands_kernel,
        (shape(WIN * LON, ROWS * LON, dtype=BF16), shape(HALO, ROWS * LON, dtype=BF16)),
        [VMEM((1184, LON), F32), VMEM((HALO, ROWS * LON), F32)],
        mem,
        taper,
    )


def split(value):
    high = value.astype(BF16)
    return high, (value - high.astype(F32)).astype(BF16)


def gathered_rows(wide, start, stride):
    parts = [wide[pl.ds(g * PART + start, GROUP, stride=stride), :] for g in range(4)]
    return jnp.concatenate(parts, 0)


def push_kernel(
    mem_ref, x_ref, c_ref, left_ref, right_ref, band_ref, out_ref, rim_ref, wide, c32, scaled, corner
):
    mem = mem_ref[0]
    wide[...] = x_ref[...].astype(F32)
    c32[...] = c_ref[...].astype(F32)
    for i in range(ROWS):
        own = gathered_rows(wide, ROWS * mem + i, CLAT) * c32[pl.ds(ROWS * mem + i, 1), :]
        high, low = split(own)
        scaled[0:MEMBERS, i * LON : (i + 1) * LON] = high
        scaled[MEMBERS:, i * LON : (i + 1) * LON] = low
    lane = lanes((MEMBERS, LON))
    east = gathered_rows(wide, GROUP * CLAT, 1) * right_ref[16:24].astype(F32)[5:6]
    west = gathered_rows(wide, GROUP * CLAT + GROUP, 1) * left_ref[16:24].astype(F32)[5:6]
    east = pltpu.roll(east, (LON - 32 * mem) % LON, 1)
    west = pltpu.roll(west, (LON + 32 - 32 * mem) % LON, 1)
    high, low = split(jnp.where(lane < 32, east, jnp.where(lane < 64, west, 0.0)))
    scaled[0:MEMBERS, ROWS * LON :] = high
    scaled[MEMBERS:, ROWS * LON :] = low
    lane = lanes((8, LON))
    corner[...] = jnp.zeros(corner.shape, BF16)
    tiles = []
    for side, ref in ((0, right_ref), (1, left_ref)):
        packed = ref[TAPE:EDGES].astype(F32)
        tiles.append(
            [
                pltpu.roll(packed[8 * (a // 4) : 8 * (a // 4) + 8], (LON + 32 * side - 32 * (a % 4)) % LON, 1)
                for a in range(SPAN)
            ]
        )
    zero = jnp.zeros((8, LON), F32)
    for j in range(WIN):
        edge = []
        for side in range(2):
            tile = zero
            for i in range(ROWS):
                if 0 <= j - i < SPAN:
                    tile = jnp.where(lane // RIM == 4 * side + i, tiles[side][j - i], tile)
            edge.append(tile)
        corner[j * LON : j * LON + 16] = jnp.concatenate([edge[1], zero], 0).astype(BF16)
        corner[j * LON + 112 : j * LON + 128] = jnp.concatenate([zero, edge[0]], 0).astype(BF16)
    unused = jnp.where(mem < 2, jnp.where(mem == 0, 12, 16), jnp.where(mem == 2, 20, 0))
    zeros = jnp.zeros((MEMBERS, LON), F32)
    for extra in range(4):
        ring = unused + extra

        @pl.when(ring < CLAT)
        def _():
            out_ref[pl.ds(ring, MEMBERS, stride=CLAT), :] = zeros

        @pl.when(ring >= CLAT)
        def _():
            rim_ref[pl.ds(ring - CLAT, MEMBERS, stride=RIM), :] = zeros

    @pl.loop(0, WIN)
    def _(j):
        at = pl.multiple_of(j * LON, LON)
        both = lax.dot_general(
            scaled[:, : ROWS * LON],
            band_ref[pl.ds(at, LON), :],
            (((1,), (1,)), ((), ())),
            preferred_element_type=F32,
        )
        both = both + lax.dot_general(
            scaled[:, ROWS * LON :],
            corner[pl.ds(at, LON), :],
            (((1,), (1,)), ((), ())),
            preferred_element_type=F32,
        )
        total = both[:MEMBERS] + both[MEMBERS:]
        ring = ring_row(mem, j)

        @pl.when(ring < CLAT)
        def _():
            out_ref[pl.ds(ring, MEMBERS, stride=CLAT), :] = total

        @pl.when(ring >= CLAT)
        def _():
            rim_ref[pl.ds(ring - CLAT, MEMBERS, stride=RIM), :] = total


def push(mem, gathered, cotangent, from_left, from_right, band):
    return call(
        push_kernel,
        (shape(MEMBERS * CLAT, LON), shape(MEMBERS * RIM, LON)),
        [
            VMEM((4 * PART, LON), F32),
            VMEM((CLAT, LON), F32),
            VMEM((2 * MEMBERS, (ROWS + 1) * LON), BF16),
            VMEM((WIN * LON, LON), BF16),
        ],
        mem,
        gathered,
        cotangent,
        from_left,
        from_right,
        band,
    )


def own_kernel(
    mem_ref, x_ref, lat_ref, v_ref, c_ref, left_ref, right_ref, band_ref, rim_ref, push_ref,
    taper_ref, out_ref,
    wide, wide_lat, v32, c32, window, own, scaled, turned, product, shifted, flat,
):
    mem = mem_ref[0]
    wide[...] = x_ref[...].astype(F32)
    wide_lat[...] = lat_ref[...].astype(F32)
    v32[...] = v_ref[...].astype(F32)
    c32[...] = c_ref[...].astype(F32)
    pad = jnp.zeros((DEPTH - MEMBERS - 1, LON), F32)
    base = MEMBERS * RIM

    def put(at, field, weight):
        high, low = split(field * weight)
        scaled[0:MEMBERS, at : at + LON] = high
        scaled[MEMBERS:, at : at + LON] = low
        whole = jnp.concatenate([field, weight, pad], 0)
        turned[at : at + LON, :] = whole.T.astype(BF16)

    for j in range(WIN):
        ring = ring_row(mem, j)

        @pl.when(ring < CLAT)
        def _():
            window[j, 0:MEMBERS] = gathered_rows(wide, ring, CLAT)
            window[j, MEMBERS : MEMBERS + 1] = v32[pl.ds(ring, 1), :]

        @pl.when(ring >= CLAT)
        def _():
            window[j, 0:MEMBERS] = wide_lat[pl.ds(ring - CLAT, MEMBERS, stride=RIM), :]
            window[j, MEMBERS : MEMBERS + 1] = wide_lat[pl.ds(base + MEMBERS + ring - CLAT, 1), :]

    for j in range(WIN):
        put(j * LON, window[j, 0:MEMBERS], window[j, MEMBERS : MEMBERS + 1])
    main = WIN * LON
    put(main, gathered_rows(wide, GROUP * CLAT, 1), right_ref[16:24].astype(F32)[4:5])
    put(main + LON, gathered_rows(wide, GROUP * CLAT + GROUP, 1), left_ref[16:24].astype(F32)[4:5])
    put(
        main + 2 * LON,
        wide_lat[base : base + MEMBERS],
        wide_lat[base + MEMBERS + RIM : base + MEMBERS + RIM + 1],
    )
    for i in range(ROWS):
        own[0:MEMBERS, i * LON : (i + 1) * LON] = gathered_rows(wide, ROWS * mem + i, CLAT).astype(BF16)
        own[MEMBERS:, i * LON : (i + 1) * LON] = jnp.zeros((DEPTH - MEMBERS, LON), BF16)
    own[:, ROWS * LON :] = jnp.where(rows_of((DEPTH, LON)) == MEMBERS, 1.0, 0.0).astype(BF16)

    both = jnp.dot(scaled[:, :main], band_ref[...], preferred_element_type=F32)
    both = both + jnp.dot(scaled[:, main:], rim_ref[...], preferred_element_type=F32)
    total = both[:MEMBERS] + both[MEMBERS:]
    share = 1.0 / (MEMBERS - 1)
    for row in range(CLAT):
        out_ref[pl.ds(row, MEMBERS, stride=CLAT), :] = push_ref[
            pl.ds(row, MEMBERS, stride=CLAT), :
        ] * (v32[row : row + 1] * share)
    for i in range(ROWS):
        at = pl.ds(ROWS * mem + i, MEMBERS, stride=CLAT)
        c_row = c32[pl.ds(ROWS * mem + i, 1), :] * share
        out_ref[at, :] = out_ref[at, :] + total[:, i * LON : (i + 1) * LON] * c_row

    step = 2 * LON
    for at in range(0, main + HALO, LON):
        product[at : at + LON] = jnp.dot(turned[at : at + LON], own[...], preferred_element_type=F32)

    lane = lanes((8, LON))
    wide_lane = lanes((24, LON))

    def diagonals(j, ring, column):
        at = pl.ds(column, LON)
        cells = [product[pl.ds(halo_row(1, ring), 8), column : column + LON]]
        for block in range(CLAT):
            cells.append(
                product[pl.ds(pl.multiple_of(j * LON + 8 * block, 8), 8), column : column + LON]
            )
        cells.append(product[pl.ds(halo_row(0, ring), 8), column : column + LON])
        for bit in (8, 4, 2, 1):
            take = (lane & (8 * bit)) != 0
            cells = [jnp.where(take, cells[s + bit], cells[s]) for s in range(len(cells) - bit)]
        taps = jnp.concatenate(cells, 0)
        for bit in (1, 2, 4):
            taps = jnp.where((wide_lane & bit) != 0, pltpu.roll(taps, 24 - bit, 0), taps)
        return taps

    def halo_row(side, ring):
        inside = side * LON + RIM * ring
        outside = 2 * LON + side * (LON // 2) + RIM * (ring - CLAT)
        return pl.multiple_of(main + jnp.where(ring < CLAT, inside, outside), 8)

    @pl.loop(0, WIN)
    def _(j):
        shifted[j] = diagonals(j, ring_row(mem, j), ROWS * LON)

    @pl.loop(0, SPAN)
    def _(a):
        for i in range(ROWS):
            taps = diagonals(a + i, ring_row(mem, a + i), i * LON)
            c_row = c32[pl.ds(ROWS * mem + i, 1), :] * share
            taps = taps * shifted[a + i] * c_row
            flat[pl.ds(a * SPAN * ROWS + i, SPAN, stride=ROWS), :] = taps[0:SPAN]

    for tap in range(TAPS):
        taper_ref[tap] = flat[tap * ROWS : tap * ROWS + ROWS]


def own_rows(mem, gathered, lat_halo, vector, cotangent, from_left, from_right, band, rim, pushed):
    return call(
        own_kernel,
        (shape(TAPS, ROWS, LON), shape(MEMBERS * CLAT, LON)),
        [
            VMEM((4 * PART, LON), F32),
            VMEM((LATROWS, LON), F32),
            VMEM((CLAT, LON), F32),
            VMEM((CLAT, LON), F32),
            VMEM((WIN, DEPTH, LON), F32),
            VMEM((DEPTH, (ROWS + 1) * LON), BF16),
            VMEM((2 * MEMBERS, WIN * LON + HALO), BF16),
            VMEM((WIN * LON + HALO, DEPTH), BF16),
            VMEM((WIN * LON + HALO, (ROWS + 1) * LON), F32),
            VMEM((WIN, 24, LON), F32),
            VMEM((TAPS * ROWS, LON), F32),
        ],
        mem,
        gathered,
        lat_halo,
        vector,
        cotangent,
        from_left,
        from_right,
        band,
        rim,
        pushed,
    )


def body(anomalies, vector, cotangent, taper):
    mem = lax.axis_index("mem")
    index = mem.astype(jnp.int32).reshape(1)
    bands_of_lat = lax.axis_size("lat")
    strips = lax.axis_size("lon")
    upper = mem < 2

    left, right = edge_messages(index, anomalies, vector, cotangent, taper)
    ring = [(i, (i + 1) % strips) for i in range(strips)]
    from_left = lax.ppermute(right, "lon", ring)
    from_right = lax.ppermute(left, "lon", [(b, a) for a, b in ring])
    band, rim = bands(index, taper)

    message = jnp.concatenate(
        [anomalies.reshape(GROUP * CLAT, LON), from_right[:GROUP], from_left[:GROUP]], 0
    )
    gathered = lax.all_gather(message, "mem", axis=0, tiled=True)

    down = [(4 * z + m, 4 * z + 4 + m) for z in range(bands_of_lat - 1) for m in (0, 1)]
    up = [(4 * z + 4 + m, 4 * z + m) for z in range(bands_of_lat - 1) for m in (2, 3)]
    groups = gathered.reshape(4, PART, LON)
    first = jnp.where(upper, RIM, 0)
    cells = lax.dynamic_slice_in_dim(
        groups[:, : GROUP * CLAT].reshape(MEMBERS, CLAT, LON), first, RIM, 1
    ).reshape(MEMBERS * RIM, LON)
    east = groups[:, GROUP * CLAT : GROUP * CLAT + GROUP].reshape(MEMBERS, LON)
    west = groups[:, GROUP * CLAT + GROUP :].reshape(MEMBERS, LON)
    east = jnp.concatenate([east, from_right[GROUP : GROUP + 1]], 0)
    west = jnp.concatenate([west, from_left[GROUP : GROUP + 1]], 0)
    half = LON // 2
    sides = jnp.where(
        upper,
        jnp.concatenate([east[:, half:], west[:, half:]], 1),
        jnp.concatenate([east[:, :half], west[:, :half]], 1),
    )
    v_rows = lax.dynamic_slice_in_dim(vector, first, RIM, 0)
    lat_message = jnp.concatenate(
        [cells, sides[:MEMBERS], v_rows, sides[MEMBERS:], jnp.zeros((7, LON), BF16)], 0
    )
    lat_halo = lax.ppermute(lat_message, ("lat", "mem"), down + up)

    pushed, pushed_out = push(index, gathered, cotangent, from_left, from_right, band)
    back = lax.ppermute(pushed_out, ("lat", "mem"), [(b, a) for a, b in down + up])

    grad_taper, partial = own_rows(
        index, gathered, lat_halo, vector, cotangent, from_left, from_right, band, rim, pushed
    )

    share = vector.astype(F32) / (MEMBERS - 1)
    back = back.reshape(MEMBERS, RIM, LON)
    none = jnp.zeros_like(back)
    placed = jnp.where(
        upper, jnp.concatenate([none, back], 1), jnp.concatenate([back, none], 1)
    )
    partial = partial.reshape(MEMBERS, CLAT, LON) + placed * share[None]
    pairs = partial.reshape(2, 2, GROUP, CLAT, LON)
    core = mem % 2
    far = mem // 2
    keep = lax.dynamic_index_in_dim(pairs, core, 1, keepdims=False)
    send = lax.dynamic_index_in_dim(pairs, 1 - core, 1, keepdims=False)
    keep = keep + lax.ppermute(send, "mem", [(0, 1), (1, 0), (2, 3), (3, 2)])
    mine = lax.dynamic_index_in_dim(keep, far, 0, keepdims=False)
    send = lax.dynamic_index_in_dim(keep, 1 - far, 0, keepdims=False)
    grad_anomalies = mine + lax.ppermute(send, "mem", [(0, 2), (2, 0), (1, 3), (3, 1)])
    return grad_taper, grad_anomalies


def solution(mesh):
    placed = (
        P("mem", "lat", "lon"),
        P("lat", "lon"),
        P("lat", "lon"),
        P(None, ("lat", "mem"), "lon"),
    )
    return jax.shard_map(
        body,
        mesh=mesh,
        in_specs=placed,
        out_specs=(P(None, ("lat", "mem"), "lon"), P("mem", "lat", "lon")),
        check_vma=False,
    )
```

```python
import jax
import jax.numpy as jnp
from jax import lax
from jax.experimental import pallas as pl
from jax.experimental.pallas import tpu as pltpu
from jax.sharding import PartitionSpec as P

SPAN = 17
RIM = 8
TAPS = SPAN * SPAN
ROWS = 4
CLAT = 16
LON = 128
WIN = ROWS + 2 * RIM
RING = CLAT + RIM
GROUP = 20
MEMBERS = 80
DEPTH = 88
CELLS = GROUP * CLAT
EDGES = 64
TAPE = 24
PART = CELLS + 2 * EDGES
HALO = 3 * LON
MAIN = WIN * LON
LATROWS = MEMBERS * RIM + MEMBERS + RIM + 8
TAPE_ROWS = 1184
F32 = jnp.float32
BF16 = jnp.bfloat16
SMEM = pltpu.SMEM
VMEM = pltpu.VMEM
SHARE = 1.0 / (MEMBERS - 1)


def lanes(shape):
    return lax.broadcasted_iota(jnp.int32, shape, len(shape) - 1)


def rows_of(shape):
    return lax.broadcasted_iota(jnp.int32, shape, len(shape) - 2)


def shape(*dims, dtype=F32):
    return jax.ShapeDtypeStruct(dims, dtype)


def call(kernel, out_shape, scratch, *args, spaces=None, limit=16, flops=0):
    if spaces is None:
        spaces = [SMEM] + [VMEM] * (len(args) - 1)
    return pl.pallas_call(
        kernel,
        out_shape=out_shape,
        in_specs=[pl.BlockSpec(memory_space=space) for space in spaces],
        out_specs=jax.tree.map(lambda _: pl.BlockSpec(memory_space=VMEM), out_shape),
        scratch_shapes=scratch,
        compiler_params=pltpu.CompilerParams(vmem_limit_bytes=limit * 2**20),
        cost_estimate=pl.CostEstimate(flops=flops, bytes_accessed=2**20, transcendentals=0),
    )(*args)


def edges_kernel(
    index_ref, own_ref, taper_ref, first_ref, second_ref, wide, fields, cells
):
    for tap in range(TAPS):
        wide[tap * ROWS : tap * ROWS + ROWS] = taper_ref[tap].astype(F32)
    wide[TAPS * ROWS :] = jnp.zeros((TAPE_ROWS - TAPS * ROWS, LON), F32)
    own = own_ref[...].astype(F32)
    fields[...] = own[CELLS:]
    cells[0 : CELLS + 2 * CLAT] = own
    cells[CELLS + 2 * CLAT :] = jnp.zeros((2 * CLAT, LON), F32)
    lane = lanes((TAPE, LON))
    left = jnp.zeros((TAPE, LON), F32)
    right = jnp.zeros((TAPE, LON), F32)
    for lat in range(CLAT):
        part = cells[pl.ds(lat, TAPE, stride=CLAT), :]
        mine = lane // RIM == lat
        left = jnp.where(mine, pltpu.roll(part, RIM * lat, 1), left)
        right = jnp.where(mine, pltpu.roll(part, (RIM * lat + RIM) % LON, 1), right)
    left_rows = [left]
    right_rows = [right]
    lane = lanes((8, LON))
    row = rows_of((8, LON))
    for block in range(5):
        left = jnp.zeros((8, LON), F32)
        right = jnp.zeros((8, LON), F32)
        for sub in range(4):
            a = block * 4 + sub
            if a >= SPAN:
                continue
            for i in range(ROWS):
                to = sub * 32 + i * RIM
                mine = lane // RIM == to // RIM
                part = wide[pl.ds(a * SPAN * ROWS + i, 8, stride=ROWS), :]
                left = jnp.where(mine, pltpu.roll(part, to, 1), left)
                part = wide[pl.ds((a * SPAN + 9) * ROWS + i, 8, stride=ROWS), :]
                right = jnp.where(mine, pltpu.roll(part, (to + RIM) % LON, 1), right)
        for bit in (1, 2, 4):
            moved = pltpu.roll(left, bit, 0)
            moved = jnp.where(row >= bit, moved, 0.0)
            left = jnp.where((lane & bit) != 0, moved, left)
            moved = pltpu.roll(right, 8 - bit, 0)
            moved = jnp.where(row < 8 - bit, moved, 0.0)
            right = jnp.where(((7 - lane) & bit) != 0, moved, right)
        left_rows.append(left)
        right_rows.append(right)
    left = jnp.concatenate(left_rows, 0)
    right = jnp.concatenate(right_rows, 0)
    odd = index_ref[3] > 0
    first_ref[...] = jnp.where(odd, right, left).astype(BF16)
    second_ref[...] = jnp.where(odd, left, right).astype(BF16)


def edge_messages(index, own, taper):
    return call(
        edges_kernel,
        (
            shape(EDGES, LON, dtype=BF16),
            shape(EDGES, LON, dtype=BF16),
            shape(TAPE_ROWS, LON),
            shape(2 * CLAT, LON),
        ),
        [VMEM(((GROUP + 4) * CLAT, LON), F32)],
        index,
        own,
        taper,
    )


def message_kernel(index_ref, own_ref, first_ref, second_ref, out_ref):
    out_ref[0:CELLS] = own_ref[0:CELLS]
    odd = index_ref[3]
    east = pl.multiple_of(CELLS + (1 - odd) * EDGES, EDGES)
    west = pl.multiple_of(CELLS + odd * EDGES, EDGES)
    out_ref[pl.ds(east, EDGES)] = first_ref[...]
    out_ref[pl.ds(west, EDGES)] = second_ref[...]


def ring_row(mem, j):
    lat = ROWS * mem - RIM + j
    return jnp.where(lat < 0, lat + RING, lat)


def halo_row(side, ring):
    inside = side * LON + RIM * ring
    outside = 2 * LON + side * (LON // 2) + RIM * (ring - CLAT)
    return jnp.where(ring < CLAT, inside, outside)


def bands_kernel(index_ref, wide, band_ref, rim_ref, narrow):
    mem = index_ref[0]
    narrow[...] = jnp.zeros(narrow.shape, F32)
    for i in range(ROWS):
        for j in range(WIN):
            if j < i or j > i + SPAN - 1:
                band_ref[j * LON : (j + 1) * LON, i * LON : (i + 1) * LON] = jnp.zeros(
                    (LON, LON), BF16
                )
    lane = lanes((24, LON))
    row = rows_of((24, LON))
    group = lanes((8, LON)) // 8
    zero = jnp.zeros((8, LON), F32)

    @pl.loop(0, SPAN)
    def _(a):
        for i in range(ROWS):
            taps = wide[pl.ds(a * SPAN * ROWS + i, 24, stride=ROWS), :]
            taps = jnp.where(row < SPAN, taps, 0.0)
            for bit in (1, 2, 4):
                taps = jnp.where((lane & bit) != 0, pltpu.roll(taps, bit, 0), taps)
            low, mid, high = taps[0:8], taps[8:16], taps[16:24]
            parts = []
            for block in range(CLAT):
                part = jnp.where(group == block, mid, zero)
                if block < 15:
                    part = jnp.where(group == block + 1, low, part)
                if block > 0:
                    part = jnp.where(group == block - 1, high, part)
                parts.append(part)
            band_ref[pl.ds(pl.multiple_of((a + i) * LON, LON), LON), i * LON : (i + 1) * LON] = (
                jnp.concatenate(parts, 0).astype(BF16)
            )
            ring = ring_row(mem, a + i)
            east = pl.multiple_of(halo_row(0, ring), 8)
            west = pl.multiple_of(halo_row(1, ring), 8)
            narrow[pl.ds(east, 8), i * LON : (i + 1) * LON] = jnp.where(group == 15, high, zero)
            narrow[pl.ds(west, 8), i * LON : (i + 1) * LON] = jnp.where(group == 0, low, zero)

    rim_ref[...] = narrow[...].astype(BF16)


def bands(index, wide):
    return call(
        bands_kernel,
        (shape(MAIN, ROWS * LON, dtype=BF16), shape(HALO, ROWS * LON, dtype=BF16)),
        [VMEM((HALO, ROWS * LON), F32)],
        index,
        wide,
    )


def split(value):
    high = value.astype(BF16)
    return high, (value - high.astype(F32)).astype(BF16)


def gathered_rows(wide, start, stride):
    parts = [wide[pl.ds(g * PART + start, GROUP, stride=stride), :] for g in range(4)]
    return jnp.concatenate(parts, 0)


def halo_cells(index_ref, wide, side):
    flip = index_ref[1 + side]
    parts = []
    for g in range(4):
        part = jnp.where(flip > 0, (g + 2) % 4, g)
        at = pl.multiple_of(part * PART + CELLS + side * EDGES, 8)
        parts.append(wide[pl.ds(at, GROUP), :])
    return jnp.concatenate(parts, 0)


def halo_field(wide, side, which):
    at = CELLS + side * EDGES + 16
    return wide[at : at + 8][4 + which : 5 + which]


def lat_kernel(index_ref, x_ref, fields, out_ref, wide, rows):
    mem = index_ref[0]
    wide[...] = x_ref[...].astype(F32)
    first = jnp.where(mem < 2, RIM, 0)
    for m in range(MEMBERS):
        at = pl.multiple_of((m // GROUP) * PART + (m % GROUP) * CLAT + first, 8)
        rows[m * RIM : m * RIM + RIM] = wide[pl.ds(at, RIM), :]
    lane = lanes((MEMBERS + 8, LON))
    pad = jnp.zeros((7, LON), F32)
    sides = []
    for side in range(2):
        cells = [halo_cells(index_ref, wide, side), halo_field(wide, side, 0), pad]
        sides.append(jnp.concatenate(cells, 0))
    half = LON // 2
    low = jnp.where(lane < half, sides[0], pltpu.roll(sides[1], half, 1))
    high = jnp.where(lane < half, pltpu.roll(sides[0], half, 1), sides[1])
    both = jnp.where(mem < 2, high, low)
    base = MEMBERS * RIM
    rows[base : base + MEMBERS] = both[:MEMBERS]
    rows[base + MEMBERS : base + MEMBERS + RIM] = fields[pl.ds(pl.multiple_of(first, 8), RIM), :]
    rows[base + MEMBERS + RIM :] = both[MEMBERS:]
    out_ref[...] = rows[...].astype(BF16)


def lat_message(index, gathered, fields):
    return call(
        lat_kernel,
        shape(LATROWS, LON, dtype=BF16),
        [VMEM((4 * PART, LON), F32), VMEM((LATROWS, LON), F32)],
        index,
        gathered,
        fields,
    )


def rim_steps(mem):
    first = jnp.where(mem < 2, 0, jnp.where(mem == 2, 4, 3))
    return first, jnp.where((mem == 0) | (mem == 3), 2, 1)


def block_steps(mem):
    first = jnp.where(mem == 0, 2, jnp.where(mem == 1, 1, 0))
    return first, jnp.where((mem == 0) | (mem == 3), 3, 4)


def pushes(scaled, corner, band_ref, step):
    at = pl.ds(pl.multiple_of(step * STEP * LON, LON), STEP * LON)
    both = lax.dot_general(
        scaled[:, : ROWS * LON],
        band_ref[at, :],
        (((1,), (1,)), ((), ())),
        preferred_element_type=F32,
    )
    both = both + lax.dot_general(
        scaled[:, ROWS * LON :],
        corner[at, :],
        (((1,), (1,)), ((), ())),
        preferred_element_type=F32,
    )
    return both[:MEMBERS] + both[MEMBERS:]


def rim_push_kernel(index_ref, x_ref, fields, band_ref, rim_ref, scaled, corner, wide):
    mem = index_ref[0]
    wide[...] = x_ref[...].astype(F32)
    for i in range(ROWS):
        own = gathered_rows(wide, ROWS * mem + i, CLAT) * fields[pl.ds(CLAT + ROWS * mem + i, 1), :]
        high, low = split(own)
        scaled[0:MEMBERS, i * LON : (i + 1) * LON] = high
        scaled[MEMBERS:, i * LON : (i + 1) * LON] = low
    lane = lanes((MEMBERS, LON))
    east = halo_cells(index_ref, wide, 0) * halo_field(wide, 0, 1)
    west = halo_cells(index_ref, wide, 1) * halo_field(wide, 1, 1)
    east = pltpu.roll(east, (LON - 32 * mem) % LON, 1)
    west = pltpu.roll(west, (LON + 32 - 32 * mem) % LON, 1)
    high, low = split(jnp.where(lane < 32, east, jnp.where(lane < 64, west, 0.0)))
    scaled[0:MEMBERS, ROWS * LON :] = high
    scaled[MEMBERS:, ROWS * LON :] = low
    lane = lanes((8, LON))
    corner[...] = jnp.zeros(corner.shape, BF16)
    tiles = []
    for side in range(2):
        part = jnp.where(index_ref[1 + side] > 0, (mem + 2) % 4, mem)
        at = pl.multiple_of(part * PART + CELLS + side * EDGES + TAPE, 8)
        packed = wide[pl.ds(at, EDGES - TAPE), :]
        tiles.append(
            [
                pltpu.roll(
                    packed[8 * (a // 4) : 8 * (a // 4) + 8],
                    (LON + 32 * side - 32 * (a % 4)) % LON,
                    1,
                )
                for a in range(SPAN)
            ]
        )
    zero = jnp.zeros((8, LON), F32)
    for j in range(WIN):
        edge = []
        for side in range(2):
            tile = zero
            for i in range(ROWS):
                if 0 <= j - i < SPAN:
                    tile = jnp.where(lane // RIM == 4 * side + i, tiles[side][j - i], tile)
            edge.append(tile)
        corner[j * LON : j * LON + 16] = jnp.concatenate([edge[1], zero], 0).astype(BF16)
        corner[j * LON + 112 : j * LON + 128] = jnp.concatenate([zero, edge[0]], 0).astype(BF16)
    zeros = jnp.zeros((MEMBERS, LON), F32)

    @pl.when((mem == 1) | (mem == 2))
    def _():
        first = jnp.where(mem == 1, 0, ROWS)
        for k in range(ROWS):
            rim_ref[pl.ds(first + k, MEMBERS, stride=RIM), :] = zeros

    first, steps = rim_steps(mem)

    @pl.loop(first, first + steps)
    def _(step):
        total = pushes(scaled, corner, band_ref, step)
        for k in range(STEP):
            row = ring_row(mem, step * STEP + k) - CLAT
            rim_ref[pl.ds(row, MEMBERS, stride=RIM), :] = total[:, k * LON : (k + 1) * LON]


def block_push_kernel(index_ref, scaled, corner, band_ref, out_ref):
    mem = index_ref[0]
    zeros = jnp.zeros((MEMBERS, LON), F32)

    @pl.when((mem == 0) | (mem == 3))
    def _():
        first = jnp.where(mem == 0, CLAT - ROWS, 0)
        for k in range(ROWS):
            out_ref[pl.ds(first + k, MEMBERS, stride=CLAT), :] = zeros

    first, steps = block_steps(mem)

    @pl.loop(first, first + steps)
    def _(step):
        total = pushes(scaled, corner, band_ref, step)
        for k in range(STEP):
            row = ring_row(mem, step * STEP + k)
            out_ref[pl.ds(row, MEMBERS, stride=CLAT), :] = total[:, k * LON : (k + 1) * LON]


STEP = 4


def rim_push(index, gathered, fields, band):
    return call(
        rim_push_kernel,
        (
            shape(MEMBERS * RIM, LON),
            shape(2 * MEMBERS, (ROWS + 1) * LON, dtype=BF16),
            shape(MAIN, LON, dtype=BF16),
        ),
        [VMEM((4 * PART, LON), F32)],
        index,
        gathered,
        fields,
        band,
        flops=4 * 10**9,
    )


def block_push(index, scaled, corner, band):
    return call(
        block_push_kernel,
        shape(MEMBERS * CLAT, LON),
        [],
        index,
        scaled,
        corner,
        band,
        flops=4 * 10**9,
    )


def first_kernel(
    index_ref, x_ref, lat_ref, fields, band_ref, rim_ref, push_ref,
    out_ref, window, halos,
    wide, wide_lat, scaled,
):
    mem = index_ref[0]
    wide[...] = x_ref[...].astype(F32)
    wide_lat[...] = lat_ref[...].astype(F32)
    base = MEMBERS * RIM
    pad = jnp.zeros((DEPTH - MEMBERS - 1, LON), F32)
    for j in range(WIN):
        ring = ring_row(mem, j)

        @pl.when(ring < CLAT)
        def _():
            window[j, 0:MEMBERS] = gathered_rows(wide, ring, CLAT)
            window[j, MEMBERS:] = jnp.concatenate([fields[pl.ds(ring, 1), :], pad], 0)

        @pl.when(ring >= CLAT)
        def _():
            window[j, 0:MEMBERS] = wide_lat[pl.ds(ring - CLAT, MEMBERS, stride=RIM), :]
            row = wide_lat[pl.ds(base + MEMBERS + ring - CLAT, 1), :]
            window[j, MEMBERS:] = jnp.concatenate([row, pad], 0)

    for side in range(2):
        halos[side, 0:MEMBERS] = halo_cells(index_ref, wide, side)
        halos[side, MEMBERS:] = jnp.concatenate([halo_field(wide, side, 0), pad], 0)
    halos[2, 0:MEMBERS] = wide_lat[base : base + MEMBERS]
    last = wide_lat[base + MEMBERS + RIM : base + MEMBERS + RIM + 1]
    halos[2, MEMBERS:] = jnp.concatenate([last, pad], 0)

    def put(at, cells):
        high, low = split(cells[0:MEMBERS] * cells[MEMBERS : MEMBERS + 1])
        scaled[0:MEMBERS, at : at + LON] = high
        scaled[MEMBERS:, at : at + LON] = low

    for j in range(WIN):
        put(j * LON, window[j])
    for k in range(3):
        put(MAIN + k * LON, halos[k])
    both = jnp.dot(scaled[:, :MAIN], band_ref[...], preferred_element_type=F32)
    both = both + jnp.dot(scaled[:, MAIN:], rim_ref[...], preferred_element_type=F32)
    total = both[:MEMBERS] + both[MEMBERS:]
    v_rows = fields[0:CLAT] * SHARE
    for m in range(MEMBERS):
        at = m * CLAT
        out_ref[at : at + CLAT] = push_ref[at : at + CLAT] * v_rows
    for i in range(ROWS):
        at = pl.ds(ROWS * mem + i, MEMBERS, stride=CLAT)
        c_row = fields[pl.ds(CLAT + ROWS * mem + i, 1), :] * SHARE
        out_ref[at, :] = out_ref[at, :] + total[:, i * LON : (i + 1) * LON] * c_row


def first_sum(index, gathered, lat_halo, fields, band, rim, pushed):
    return call(
        first_kernel,
        (shape(MEMBERS * CLAT, LON), shape(WIN, DEPTH, LON), shape(3, DEPTH, LON)),
        [
            VMEM((4 * PART, LON), F32),
            VMEM((LATROWS, LON), F32),
            VMEM((2 * MEMBERS, MAIN + HALO), BF16),
        ],
        index,
        gathered,
        lat_halo,
        fields,
        band,
        rim,
        pushed,
        flops=4 * 10**9,
    )


def near_kernel(index_ref, part_ref, back_ref, fields, keep_ref, send_ref):
    mem = index_ref[0]
    core = mem % 2
    first = pl.multiple_of(jnp.where(mem < 2, RIM, 0), 8)
    v_rows = fields[pl.ds(first, RIM), :] * SHARE
    for half in range(2):
        for take, target in ((core, keep_ref), (1 - core, send_ref)):
            at = pl.multiple_of((2 * half + take) * CELLS, 8)
            target[half * CELLS : (half + 1) * CELLS] = part_ref[pl.ds(at, CELLS), :]
            at = pl.multiple_of((2 * half + take) * GROUP * RIM, 8)
            more = back_ref[pl.ds(at, GROUP * RIM), :]
            for m in range(GROUP):
                to = pl.ds(pl.multiple_of(half * CELLS + m * CLAT + first, 8), RIM)
                target[to, :] = target[to, :] + more[m * RIM : (m + 1) * RIM] * v_rows


def near_parts(index, partial, back, fields):
    return call(
        near_kernel,
        (shape(2 * CELLS, LON), shape(2 * CELLS, LON)),
        [],
        index,
        partial,
        back,
        fields,
    )


def far_kernel(index_ref, keep_ref, more_ref, mine_ref, send_ref):
    far = index_ref[0] // 2
    at = pl.ds(pl.multiple_of(far * CELLS, 8), CELLS)
    mine_ref[...] = keep_ref[at, :] + more_ref[at, :]
    at = pl.ds(pl.multiple_of((1 - far) * CELLS, 8), CELLS)
    send = keep_ref[at, :] + more_ref[at, :]
    largest = jnp.full((16, LON), jnp.max(jnp.abs(send)), F32)
    power = jnp.clip(jnp.round(jnp.log2(largest)) - 8.0, -120.0, 100.0)
    send_ref[0:CELLS] = send * jnp.exp2(-power)[0:1]
    send_ref[CELLS:] = power


def far_parts(index, keep, more):
    return call(far_kernel, (shape(CELLS, LON), shape(CELLS + 16, LON)), [], index, keep, more)


def taper_part(index_ref, window, halos, fields, flat, own, turned, product, shifted, taps_of):
    mem = index_ref[0]
    used = range(taps_of[0], taps_of[-1] + ROWS)
    for j in used:
        turned[j * LON : (j + 1) * LON, :] = window[j].T.astype(BF16)
    for k in range(3):
        turned[MAIN + k * LON : MAIN + (k + 1) * LON, :] = halos[k].T.astype(BF16)
    keep = rows_of((DEPTH, LON)) < MEMBERS
    for i in range(ROWS):
        own[:, i * LON : (i + 1) * LON] = jnp.where(keep, window[RIM + i], 0.0).astype(BF16)
    own[:, ROWS * LON :] = jnp.where(rows_of((DEPTH, LON)) == MEMBERS, 1.0, 0.0).astype(BF16)
    for j in [*used, WIN, WIN + 1, WIN + 2]:
        at = j * LON
        product[at : at + LON] = jnp.dot(turned[at : at + LON], own[...], preferred_element_type=F32)
    lane = lanes((8, LON))
    wide_lane = lanes((24, LON))

    def diagonals(j, column):
        ring = ring_row(mem, j)
        east = pl.multiple_of(MAIN + halo_row(0, ring), 8)
        west = pl.multiple_of(MAIN + halo_row(1, ring), 8)
        cells = [product[pl.ds(west, 8), column : column + LON]]
        for block in range(CLAT):
            at = pl.multiple_of(j * LON + 8 * block, 8)
            cells.append(product[pl.ds(at, 8), column : column + LON])
        cells.append(product[pl.ds(east, 8), column : column + LON])
        for bit in (8, 4, 2, 1):
            take = (lane & (8 * bit)) != 0
            cells = [jnp.where(take, cells[s + bit], cells[s]) for s in range(len(cells) - bit)]
        taps = jnp.concatenate(cells, 0)
        for bit in (1, 2, 4):
            taps = jnp.where((wide_lane & bit) != 0, pltpu.roll(taps, 24 - bit, 0), taps)
        return taps

    @pl.loop(used[0], used[-1] + 1)
    def _(j):
        shifted[j] = diagonals(j, ROWS * LON)

    @pl.loop(taps_of[0], taps_of[-1] + 1)
    def _(a):
        for i in range(ROWS):
            c_row = fields[pl.ds(CLAT + ROWS * mem + i, 1), :] * SHARE
            taps = diagonals(a + i, i * LON) * shifted[a + i] * c_row
            flat[pl.ds(a * SPAN * ROWS + i, SPAN, stride=ROWS), :] = taps[0:SPAN]


EARLY = 9


def early_kernel(index_ref, window, halos, fields, flat, *scratch):
    taper_part(index_ref, window, halos, fields, flat, *scratch, range(EARLY))


def late_kernel(index_ref, window, halos, fields, early, taper_ref, flat, *scratch):
    taper_part(index_ref, window, halos, fields, flat, *scratch, range(EARLY, SPAN))
    for tap in range(TAPS):
        source = early if tap < EARLY * SPAN else flat
        taper_ref[tap] = source[tap * ROWS : tap * ROWS + ROWS]


def taper_scratch():
    return [
        VMEM((DEPTH, (ROWS + 1) * LON), BF16),
        VMEM((MAIN + HALO, DEPTH), BF16),
        VMEM((MAIN + HALO, (ROWS + 1) * LON), F32),
        VMEM((WIN, 24, LON), F32),
    ]


def early_taps(index, window, halos, fields):
    return call(
        early_kernel, shape(EARLY * SPAN * ROWS, LON), taper_scratch(),
        index, window, halos, fields, limit=24, flops=3 * 10**9,
    )


def late_taps(index, window, halos, fields, early):
    return call(
        late_kernel, shape(TAPS, ROWS, LON), [VMEM((TAPS * ROWS, LON), F32), *taper_scratch()],
        index, window, halos, fields, early, limit=24, flops=3 * 10**9,
    )


def body(anomalies, vector, cotangent, taper):
    mem = lax.axis_index("mem").astype(jnp.int32)
    strip = lax.axis_index("lon")
    blocks = lax.axis_size("lat")
    strips = lax.axis_size("lon")
    index = jnp.stack(
        [
            mem,
            (strip == strips - 1).astype(jnp.int32),
            (strip == 0).astype(jnp.int32),
            (strip % 2).astype(jnp.int32),
        ]
    )
    own = jnp.concatenate([anomalies.reshape(CELLS, LON), vector, cotangent], 0)
    first, second, wide, fields = edge_messages(index, own, taper)
    swaps = ([], [])
    for s in range(strips):
        for m in range(4):
            here = 4 * s + m
            there = here + 4 if s < strips - 1 else (m + 2) % 4
            swaps[1 - s % 2].extend([(here, there), (there, here)])
    first = lax.ppermute(first, ("lon", "mem"), swaps[0])
    second = lax.ppermute(second, ("lon", "mem"), swaps[1])
    band, rim = bands(index, wide)
    first, second, band, rim = lax.optimization_barrier((first, second, band, rim))
    message = call(
        message_kernel, shape(PART, LON, dtype=BF16), [], index, own, first, second
    )
    gathered = lax.all_gather(message, "mem", axis=0, tiled=True)

    down = [(4 * z + m, 4 * z + 4 + m) for z in range(blocks - 1) for m in (0, 1)]
    up = [(4 * z + 4 + m, 4 * z + m) for z in range(blocks - 1) for m in (2, 3)]
    message = lat_message(index, gathered, fields)
    message, gathered = lax.optimization_barrier((message, gathered))
    lat_halo = lax.ppermute(message, ("lat", "mem"), down + up)
    pushed_out, scaled, corner = rim_push(index, gathered, fields, band)
    back = lax.ppermute(pushed_out, ("lat", "mem"), [(b, a) for a, b in down + up])
    pushed = block_push(index, scaled, corner, band)
    partial, window, halos = first_sum(index, gathered, lat_halo, fields, band, rim, pushed)
    early = early_taps(index, window, halos, fields)
    back, early = lax.optimization_barrier((back, early))
    keep, send = near_parts(index, partial, back, fields)
    more = lax.ppermute(send, "mem", [(0, 1), (1, 0), (2, 3), (3, 2)])
    mine, send = far_parts(index, keep, more)
    half = lax.ppermute(send.astype(jnp.float16), "mem", [(0, 2), (2, 0), (1, 3), (3, 1)])
    mine, early = lax.optimization_barrier((mine, early))
    grad_taper = late_taps(index, window, halos, fields, early)
    more = half.astype(F32)
    grad_anomalies = mine + more[:CELLS] * jnp.exp2(more[CELLS : CELLS + 1])
    grad_anomalies = grad_anomalies.reshape(GROUP, CLAT, LON)
    return grad_taper, grad_anomalies


def solution(mesh):
    placed = (
        P("mem", "lat", "lon"),
        P("lat", "lon"),
        P("lat", "lon"),
        P(None, ("lat", "mem"), "lon"),
    )
    return jax.shard_map(
        body,
        mesh=mesh,
        in_specs=placed,
        out_specs=(P(None, ("lat", "mem"), "lon"), P("mem", "lat", "lon")),
        check_vma=False,
    )
```

```python
import jax
import jax.numpy as jnp
from jax import lax
from jax.experimental import pallas as pl
from jax.experimental.pallas import tpu as pltpu
from jax.sharding import PartitionSpec as P

SPAN = 17
RIM = 8
TAPS = SPAN * SPAN
ROWS = 4
CLAT = 16
LON = 128
WIN = ROWS + 2 * RIM
RING = CLAT + RIM
GROUP = 20
MEMBERS = 80
DEPTH = 88
CELLS = GROUP * CLAT
EDGES = 64
TAPE = 24
PART = CELLS + 2 * EDGES
HALO = 3 * LON
MAIN = WIN * LON
BACK = MEMBERS * RIM
LATROWS = MEMBERS * RIM + MEMBERS + RIM + 8
TAPE_ROWS = 1184
F32 = jnp.float32
BF16 = jnp.bfloat16
VMEM = pltpu.VMEM
SHARE = 1.0 / (MEMBERS - 1)


def lanes(shape):
    return lax.broadcasted_iota(jnp.int32, shape, len(shape) - 1)


def rows_of(shape):
    return lax.broadcasted_iota(jnp.int32, shape, len(shape) - 2)


def shape(*dims, dtype=F32):
    return jax.ShapeDtypeStruct(dims, dtype)


def call(kernel, out_shape, scratch, *args, limit=16, flops=0):
    return pl.pallas_call(
        kernel,
        out_shape=out_shape,
        in_specs=[pl.BlockSpec(memory_space=VMEM)] * len(args),
        out_specs=jax.tree.map(lambda _: pl.BlockSpec(memory_space=VMEM), out_shape),
        scratch_shapes=scratch,
        compiler_params=pltpu.CompilerParams(vmem_limit_bytes=limit * 2**20),
        cost_estimate=pl.CostEstimate(flops=flops, bytes_accessed=2**20, transcendentals=0),
    )(*args)


def edges_kernel(
    own_ref, taper_ref, first_ref, second_ref, wide, fields, cells
):
    for tap in range(TAPS):
        wide[tap * ROWS : tap * ROWS + ROWS] = taper_ref[tap].astype(F32)
    wide[TAPS * ROWS :] = jnp.zeros((TAPE_ROWS - TAPS * ROWS, LON), F32)
    own = own_ref[...].astype(F32)
    fields[...] = own[CELLS:]
    cells[0 : CELLS + 2 * CLAT] = own
    cells[CELLS + 2 * CLAT :] = jnp.zeros((2 * CLAT, LON), F32)
    lane = lanes((TAPE, LON))
    left = jnp.zeros((TAPE, LON), F32)
    right = jnp.zeros((TAPE, LON), F32)
    for lat in range(CLAT):
        part = cells[pl.ds(lat, TAPE, stride=CLAT), :]
        mine = lane // RIM == lat
        left = jnp.where(mine, pltpu.roll(part, RIM * lat, 1), left)
        right = jnp.where(mine, pltpu.roll(part, (RIM * lat + RIM) % LON, 1), right)
    left_rows = [left]
    right_rows = [right]
    lane = lanes((8, LON))
    row = rows_of((8, LON))
    for block in range(5):
        left = jnp.zeros((8, LON), F32)
        right = jnp.zeros((8, LON), F32)
        for sub in range(4):
            a = block * 4 + sub
            if a >= SPAN:
                continue
            for i in range(ROWS):
                to = sub * 32 + i * RIM
                mine = lane // RIM == to // RIM
                part = wide[pl.ds(a * SPAN * ROWS + i, 8, stride=ROWS), :]
                left = jnp.where(mine, pltpu.roll(part, to, 1), left)
                part = wide[pl.ds((a * SPAN + 9) * ROWS + i, 8, stride=ROWS), :]
                right = jnp.where(mine, pltpu.roll(part, (to + RIM) % LON, 1), right)
        for bit in (1, 2, 4):
            moved = pltpu.roll(left, bit, 0)
            moved = jnp.where(row >= bit, moved, 0.0)
            left = jnp.where((lane & bit) != 0, moved, left)
            moved = pltpu.roll(right, 8 - bit, 0)
            moved = jnp.where(row < 8 - bit, moved, 0.0)
            right = jnp.where(((7 - lane) & bit) != 0, moved, right)
        left_rows.append(left)
        right_rows.append(right)
    left = jnp.concatenate(left_rows, 0)
    right = jnp.concatenate(right_rows, 0)
    odd = lax.axis_index("lon") % 2 == 1
    first_ref[...] = jnp.where(odd, right, left).astype(BF16)
    second_ref[...] = jnp.where(odd, left, right).astype(BF16)


def edge_messages(own, taper):
    return call(
        edges_kernel,
        (
            shape(EDGES, LON, dtype=BF16),
            shape(EDGES, LON, dtype=BF16),
            shape(TAPE_ROWS, LON),
            shape(2 * CLAT, LON),
        ),
        [VMEM(((GROUP + 4) * CLAT, LON), F32)],
        own,
        taper,
    )


def message_kernel(own_ref, first_ref, second_ref, out_ref):
    out_ref[0:CELLS] = own_ref[0:CELLS]
    odd = lax.axis_index("lon") % 2
    east = pl.multiple_of(CELLS + (1 - odd) * EDGES, EDGES)
    west = pl.multiple_of(CELLS + odd * EDGES, EDGES)
    out_ref[pl.ds(east, EDGES)] = first_ref[...]
    out_ref[pl.ds(west, EDGES)] = second_ref[...]


def ring_row(mem, j):
    lat = ROWS * mem - RIM + j
    return jnp.where(lat < 0, lat + RING, lat)


def halo_row(side, ring):
    inside = side * LON + RIM * ring
    outside = 2 * LON + side * (LON // 2) + RIM * (ring - CLAT)
    return jnp.where(ring < CLAT, inside, outside)


def bands_kernel(wide, band_ref, rim_ref, narrow):
    mem = lax.axis_index("mem")
    narrow[...] = jnp.zeros(narrow.shape, F32)
    for i in range(ROWS):
        for j in range(WIN):
            if j < i or j > i + SPAN - 1:
                band_ref[j * LON : (j + 1) * LON, i * LON : (i + 1) * LON] = jnp.zeros(
                    (LON, LON), BF16
                )
    lane = lanes((24, LON))
    row = rows_of((24, LON))
    group = lanes((8, LON)) // 8
    zero = jnp.zeros((8, LON), F32)

    @pl.loop(0, SPAN)
    def _(a):
        for i in range(ROWS):
            taps = wide[pl.ds(a * SPAN * ROWS + i, 24, stride=ROWS), :]
            taps = jnp.where(row < SPAN, taps, 0.0)
            for bit in (1, 2, 4):
                taps = jnp.where((lane & bit) != 0, pltpu.roll(taps, bit, 0), taps)
            low, mid, high = taps[0:8], taps[8:16], taps[16:24]
            parts = []
            for block in range(CLAT):
                part = jnp.where(group == block, mid, zero)
                if block < 15:
                    part = jnp.where(group == block + 1, low, part)
                if block > 0:
                    part = jnp.where(group == block - 1, high, part)
                parts.append(part)
            band_ref[pl.ds(pl.multiple_of((a + i) * LON, LON), LON), i * LON : (i + 1) * LON] = (
                jnp.concatenate(parts, 0).astype(BF16)
            )
            ring = ring_row(mem, a + i)
            east = pl.multiple_of(halo_row(0, ring), 8)
            west = pl.multiple_of(halo_row(1, ring), 8)
            narrow[pl.ds(east, 8), i * LON : (i + 1) * LON] = jnp.where(group == 15, high, zero)
            narrow[pl.ds(west, 8), i * LON : (i + 1) * LON] = jnp.where(group == 0, low, zero)

    rim_ref[...] = narrow[...].astype(BF16)


def bands(wide):
    return call(
        bands_kernel,
        (shape(MAIN, ROWS * LON, dtype=BF16), shape(HALO, ROWS * LON, dtype=BF16)),
        [VMEM((HALO, ROWS * LON), F32)],
        wide,
    )


def split(value):
    high = value.astype(BF16)
    return high, (value - high.astype(F32)).astype(BF16)


def gathered_rows(wide, start, stride):
    parts = [wide[pl.ds(g * PART + start, GROUP, stride=stride), :] for g in range(4)]
    return jnp.concatenate(parts, 0)


def over_seam(side):
    last = lax.axis_size("lon") - 1
    return lax.axis_index("lon") == (0 if side else last)


def halo_cells(wide, side, pitch=PART):
    flip = over_seam(side)
    parts = []
    for g in range(4):
        part = jnp.where(flip, (g + 2) % 4, g)
        at = pl.multiple_of(part * pitch + pitch - 2 * EDGES + side * EDGES, 8)
        parts.append(wide[pl.ds(at, GROUP), :])
    return jnp.concatenate(parts, 0)


def halo_field(wide, side, which, pitch=PART):
    at = pitch - 2 * EDGES + side * EDGES + 16
    return wide[at : at + 8][4 + which : 5 + which]


def lat_kernel(x_ref, fields, out_ref, halos, rows):
    mem = lax.axis_index("mem")
    upper = mem < 2
    first = jnp.where(upper, RIM, 0)
    for m in range(0, MEMBERS, 2):
        at = (m // GROUP) * PART + (m % GROUP) * CLAT
        pair = x_ref[at : at + 2 * CLAT].astype(F32)
        one = jnp.where(upper, pair[RIM:CLAT], pair[0:RIM])
        two = jnp.where(upper, pair[CLAT + RIM :], pair[CLAT : CLAT + RIM])
        out_ref[m * RIM : m * RIM + CLAT] = jnp.concatenate([one, two], 0).astype(BF16)
    for g in range(4):
        at = g * 2 * EDGES
        halos[at : at + 2 * EDGES] = x_ref[g * PART + CELLS : (g + 1) * PART].astype(F32)
    lane = lanes((MEMBERS + 8, LON))
    pad = jnp.zeros((7, LON), F32)
    sides = []
    for side in range(2):
        cells = [
            halo_cells(halos, side, 2 * EDGES),
            halo_field(halos, side, 0, 2 * EDGES),
            pad,
        ]
        sides.append(jnp.concatenate(cells, 0))
    half = LON // 2
    low = jnp.where(lane < half, sides[0], pltpu.roll(sides[1], half, 1))
    high = jnp.where(lane < half, pltpu.roll(sides[0], half, 1), sides[1])
    both = jnp.where(mem < 2, high, low)
    rows[0:MEMBERS] = both[:MEMBERS]
    rows[MEMBERS : MEMBERS + RIM] = fields[pl.ds(pl.multiple_of(first, 8), RIM), :]
    rows[MEMBERS + RIM :] = both[MEMBERS:]
    out_ref[MEMBERS * RIM :] = rows[...].astype(BF16)


def lat_message(gathered, fields):
    return call(
        lat_kernel,
        shape(LATROWS, LON, dtype=BF16),
        [VMEM((8 * EDGES, LON), F32), VMEM((LATROWS - MEMBERS * RIM, LON), F32)],
        gathered,
        fields,
    )


def rim_steps(mem):
    first = jnp.where(mem < 2, 0, jnp.where(mem == 2, 4, 3))
    return first, jnp.where((mem == 0) | (mem == 3), 2, 1)


def block_steps(mem):
    first = jnp.where(mem == 0, 2, jnp.where(mem == 1, 1, 0))
    return first, jnp.where((mem == 0) | (mem == 3), 3, 4)


def pushes(scaled, corner, band_ref, step):
    at = pl.ds(pl.multiple_of(step * STEP * LON, LON), STEP * LON)
    both = lax.dot_general(
        scaled[:, : ROWS * LON],
        band_ref[at, :],
        (((1,), (1,)), ((), ())),
        preferred_element_type=F32,
    )
    both = both + lax.dot_general(
        scaled[:, ROWS * LON :],
        corner[at, :],
        (((1,), (1,)), ((), ())),
        preferred_element_type=F32,
    )
    return both[:MEMBERS] + both[MEMBERS:]


def by_core(mem, members):
    even = jnp.concatenate([members[0:GROUP], members[2 * GROUP : 3 * GROUP]], 0)
    odd = jnp.concatenate([members[GROUP : 2 * GROUP], members[3 * GROUP :]], 0)
    first = mem % 2 == 0
    return jnp.where(first, even, odd), jnp.where(first, odd, even)


def scale_down(ref, rows):
    values = ref[0:rows]
    largest = jnp.full((16, LON), jnp.max(jnp.abs(values)), F32)
    power = jnp.clip(jnp.round(jnp.log2(largest)) - 8.0, -120.0, 100.0)
    ref[0:rows] = values * jnp.exp2(-power)[0:1]
    ref[rows : rows + 16] = power


def rim_push_kernel(x_ref, fields, band_ref, rim_ref, scaled, corner, wide):
    mem = lax.axis_index("mem")
    wide[...] = x_ref[...].astype(F32)
    for i in range(ROWS):
        own = gathered_rows(wide, ROWS * mem + i, CLAT) * fields[pl.ds(CLAT + ROWS * mem + i, 1), :]
        high, low = split(own)
        scaled[0:MEMBERS, i * LON : (i + 1) * LON] = high
        scaled[MEMBERS:, i * LON : (i + 1) * LON] = low
    lane = lanes((MEMBERS, LON))
    east = halo_cells(wide, 0) * halo_field(wide, 0, 1)
    west = halo_cells(wide, 1) * halo_field(wide, 1, 1)
    east = pltpu.roll(east, (LON - 32 * mem) % LON, 1)
    west = pltpu.roll(west, (LON + 32 - 32 * mem) % LON, 1)
    high, low = split(jnp.where(lane < 32, east, jnp.where(lane < 64, west, 0.0)))
    scaled[0:MEMBERS, ROWS * LON :] = high
    scaled[MEMBERS:, ROWS * LON :] = low
    lane = lanes((8, LON))
    corner[...] = jnp.zeros(corner.shape, BF16)
    tiles = []
    for side in range(2):
        part = jnp.where(over_seam(side), (mem + 2) % 4, mem)
        at = pl.multiple_of(part * PART + CELLS + side * EDGES + TAPE, 8)
        packed = wide[pl.ds(at, EDGES - TAPE), :]
        tiles.append(
            [
                pltpu.roll(
                    packed[8 * (a // 4) : 8 * (a // 4) + 8],
                    (LON + 32 * side - 32 * (a % 4)) % LON,
                    1,
                )
                for a in range(SPAN)
            ]
        )
    zero = jnp.zeros((8, LON), F32)
    for j in range(WIN):
        edge = []
        for side in range(2):
            tile = zero
            for i in range(ROWS):
                if 0 <= j - i < SPAN:
                    tile = jnp.where(lane // RIM == 4 * side + i, tiles[side][j - i], tile)
            edge.append(tile)
        corner[j * LON : j * LON + 16] = jnp.concatenate([edge[1], zero], 0).astype(BF16)
        corner[j * LON + 112 : j * LON + 128] = jnp.concatenate([zero, edge[0]], 0).astype(BF16)
    zeros = jnp.zeros((MEMBERS, LON), F32)

    @pl.when((mem == 1) | (mem == 2))
    def _():
        first = jnp.where(mem == 1, 0, ROWS)
        for k in range(ROWS):
            rim_ref[pl.ds(first + k, MEMBERS, stride=RIM), :] = zeros

    first, steps = rim_steps(mem)

    @pl.loop(first, first + steps)
    def _(step):
        total = pushes(scaled, corner, band_ref, step)
        for k in range(STEP):
            row = pl.ds(ring_row(mem, step * STEP + k) - CLAT, MEMBERS, stride=RIM)
            rim_ref[row, :] = total[:, k * LON : (k + 1) * LON]

    scale_down(rim_ref, BACK)


def block_push_kernel(scaled, corner, band_ref, out_ref):
    mem = lax.axis_index("mem")
    zeros = jnp.zeros((MEMBERS, LON), F32)

    @pl.when((mem == 0) | (mem == 3))
    def _():
        first = jnp.where(mem == 0, CLAT - ROWS, 0)
        for k in range(ROWS):
            out_ref[pl.ds(first + k, MEMBERS, stride=CLAT), :] = zeros

    first, steps = block_steps(mem)

    @pl.loop(first, first + steps)
    def _(step):
        total = pushes(scaled, corner, band_ref, step)
        for k in range(STEP):
            row = ring_row(mem, step * STEP + k)
            out_ref[pl.ds(row, MEMBERS, stride=CLAT), :] = total[:, k * LON : (k + 1) * LON]


STEP = 4


def rim_push(gathered, fields, band):
    return call(
        rim_push_kernel,
        (
            shape(BACK + 16, LON),
            shape(2 * MEMBERS, (ROWS + 1) * LON, dtype=BF16),
            shape(MAIN, LON, dtype=BF16),
            shape(4 * PART, LON),
        ),
        [],
        gathered,
        fields,
        band,
        flops=10**6,
    )


def block_push(scaled, corner, band):
    return call(
        block_push_kernel,
        shape(MEMBERS * CLAT, LON),
        [],
        scaled,
        corner,
        band,
        flops=10**6,
    )


def first_kernel(
    wide, lat_ref, fields, band_ref, rim_ref, push_ref,
    keep_ref, send_ref, window, halos,
    wide_lat, scaled,
):
    mem = lax.axis_index("mem")
    wide_lat[...] = lat_ref[...].astype(F32)
    base = MEMBERS * RIM
    pad = jnp.zeros((DEPTH - MEMBERS - 1, LON), F32)
    for j in range(WIN):
        ring = ring_row(mem, j)

        @pl.when(ring < CLAT)
        def _():
            window[j, 0:MEMBERS] = gathered_rows(wide, ring, CLAT)
            window[j, MEMBERS:] = jnp.concatenate([fields[pl.ds(ring, 1), :], pad], 0)

        @pl.when(ring >= CLAT)
        def _():
            window[j, 0:MEMBERS] = wide_lat[pl.ds(ring - CLAT, MEMBERS, stride=RIM), :]
            row = wide_lat[pl.ds(base + MEMBERS + ring - CLAT, 1), :]
            window[j, MEMBERS:] = jnp.concatenate([row, pad], 0)

    for side in range(2):
        halos[side, 0:MEMBERS] = halo_cells(wide, side)
        halos[side, MEMBERS:] = jnp.concatenate([halo_field(wide, side, 0), pad], 0)
    halos[2, 0:MEMBERS] = wide_lat[base : base + MEMBERS]
    last = wide_lat[base + MEMBERS + RIM : base + MEMBERS + RIM + 1]
    halos[2, MEMBERS:] = jnp.concatenate([last, pad], 0)

    def put(at, cells):
        high, low = split(cells[0:MEMBERS] * cells[MEMBERS : MEMBERS + 1])
        scaled[0:MEMBERS, at : at + LON] = high
        scaled[MEMBERS:, at : at + LON] = low

    for j in range(WIN):
        put(j * LON, window[j])
    for k in range(3):
        put(MAIN + k * LON, halos[k])
    both = jnp.dot(scaled[:, :MAIN], band_ref[...], preferred_element_type=F32)
    both = both + jnp.dot(scaled[:, MAIN:], rim_ref[...], preferred_element_type=F32)
    total = both[:MEMBERS] + both[MEMBERS:]
    v_rows = fields[0:CLAT] * SHARE
    core = mem % 2
    for half in range(2):
        for take, target in ((core, keep_ref), (1 - core, send_ref)):
            for m in range(GROUP):
                at = pl.multiple_of((2 * half + take) * CELLS + m * CLAT, 8)
                to = half * CELLS + m * CLAT
                target[to : to + CLAT] = push_ref[pl.ds(at, CLAT), :] * v_rows
    for i in range(ROWS):
        at = pl.ds(ROWS * mem + i, 2 * GROUP, stride=CLAT)
        c_row = fields[pl.ds(CLAT + ROWS * mem + i, 1), :] * SHARE
        keep, send = by_core(mem, total[:, i * LON : (i + 1) * LON] * c_row)
        keep_ref[at, :] = keep_ref[at, :] + keep
        send_ref[at, :] = send_ref[at, :] + send


def first_sum(wide, lat_halo, fields, band, rim, pushed):
    return call(
        first_kernel,
        (
            shape(2 * CELLS, LON),
            shape(2 * CELLS, LON),
            shape(WIN, DEPTH, LON),
            shape(3, DEPTH, LON),
        ),
        [
            VMEM((LATROWS, LON), F32),
            VMEM((2 * MEMBERS, MAIN + HALO), BF16),
        ],
        wide,
        lat_halo,
        fields,
        band,
        rim,
        pushed,
        flops=10**6,
    )


def add_back(mem, take, half, at, back_ref, fields, target):
    first = jnp.where(mem < 2, RIM, 0)
    rows = fields[pl.ds(pl.multiple_of(first, 8), RIM), :] * SHARE
    rows = rows * jnp.exp2(back_ref[BACK : BACK + 1])
    start = (2 * half + take) * GROUP * RIM
    for m in range(GROUP):
        source = pl.ds(pl.multiple_of(start + m * RIM, 8), RIM)
        to = pl.ds(pl.multiple_of(at + m * CLAT + first, 8), RIM)
        target[to, :] = target[to, :] + back_ref[source, :] * rows


def near_kernel(part_ref, back_ref, fields, send_ref):
    mem = lax.axis_index("mem")
    send_ref[...] = part_ref[...]
    for half in range(2):
        add_back(mem, 1 - mem % 2, half, half * CELLS, back_ref, fields, send_ref)


def near_parts(part, back, fields):
    return call(near_kernel, shape(2 * CELLS, LON), [], part, back, fields)


def far_kernel(keep_ref, more_ref, back_ref, fields, mine_ref, send_ref):
    mem = lax.axis_index("mem")
    far = mem // 2
    for take, target in ((far, mine_ref), (1 - far, send_ref)):
        at = pl.ds(pl.multiple_of(take * CELLS, 8), CELLS)
        target[0:CELLS] = keep_ref[at, :] + more_ref[at, :]
        add_back(mem, mem % 2, take, 0, back_ref, fields, target)
    scale_down(send_ref, CELLS)


def far_parts(keep, more, back, fields):
    return call(
        far_kernel, (shape(CELLS, LON), shape(CELLS + 16, LON)), [],
        keep, more, back, fields,
    )


def taper_part(window, halos, fields, flat, own, turned, product, shifted, taps_of):
    mem = lax.axis_index("mem")
    used = range(taps_of[0], taps_of[-1] + ROWS)
    for j in used:
        turned[j * LON : (j + 1) * LON, :] = window[j].T.astype(BF16)
    for k in range(3):
        turned[MAIN + k * LON : MAIN + (k + 1) * LON, :] = halos[k].T.astype(BF16)
    keep = rows_of((DEPTH, LON)) < MEMBERS
    for i in range(ROWS):
        own[:, i * LON : (i + 1) * LON] = jnp.where(keep, window[RIM + i], 0.0).astype(BF16)
    own[:, ROWS * LON :] = jnp.where(rows_of((DEPTH, LON)) == MEMBERS, 1.0, 0.0).astype(BF16)
    for j in [*used, WIN, WIN + 1, WIN + 2]:
        at = j * LON
        product[at : at + LON] = jnp.dot(turned[at : at + LON], own[...], preferred_element_type=F32)
    lane = lanes((8, LON))
    wide_lane = lanes((24, LON))

    def diagonals(j, column):
        ring = ring_row(mem, j)
        east = pl.multiple_of(MAIN + halo_row(0, ring), 8)
        west = pl.multiple_of(MAIN + halo_row(1, ring), 8)
        cells = [product[pl.ds(west, 8), column : column + LON]]
        for block in range(CLAT):
            at = pl.multiple_of(j * LON + 8 * block, 8)
            cells.append(product[pl.ds(at, 8), column : column + LON])
        cells.append(product[pl.ds(east, 8), column : column + LON])
        for bit in (8, 4, 2, 1):
            take = (lane & (8 * bit)) != 0
            cells = [jnp.where(take, cells[s + bit], cells[s]) for s in range(len(cells) - bit)]
        taps = jnp.concatenate(cells, 0)
        for bit in (1, 2, 4):
            taps = jnp.where((wide_lane & bit) != 0, pltpu.roll(taps, 24 - bit, 0), taps)
        return taps

    @pl.loop(used[0], used[-1] + 1)
    def _(j):
        shifted[j] = diagonals(j, ROWS * LON)

    @pl.loop(taps_of[0], taps_of[-1] + 1)
    def _(a):
        for i in range(ROWS):
            c_row = fields[pl.ds(CLAT + ROWS * mem + i, 1), :] * SHARE
            taps = diagonals(a + i, i * LON) * shifted[a + i] * c_row
            flat[pl.ds(a * SPAN * ROWS + i, SPAN, stride=ROWS), :] = taps[0:SPAN]


EARLY = 2


def early_kernel(window, halos, fields, flat, *scratch):
    taper_part(window, halos, fields, flat, *scratch, range(EARLY))


def late_kernel(window, halos, fields, early, taper_ref, flat, *scratch):
    taper_part(window, halos, fields, flat, *scratch, range(EARLY, SPAN))
    for tap in range(TAPS):
        source = early if tap < EARLY * SPAN else flat
        taper_ref[tap] = source[tap * ROWS : tap * ROWS + ROWS]


def taper_scratch():
    return [
        VMEM((DEPTH, (ROWS + 1) * LON), BF16),
        VMEM((MAIN + HALO, DEPTH), BF16),
        VMEM((MAIN + HALO, (ROWS + 1) * LON), F32),
        VMEM((WIN, 24, LON), F32),
    ]


def early_taps(window, halos, fields):
    return call(
        early_kernel, shape(EARLY * SPAN * ROWS, LON), taper_scratch(),
        window, halos, fields, limit=24, flops=2 * 10**10,
    )


def late_taps(window, halos, fields, early):
    return call(
        late_kernel, shape(TAPS, ROWS, LON), [VMEM((TAPS * ROWS, LON), F32), *taper_scratch()],
        window, halos, fields, early, limit=24, flops=10**6,
    )


def body(anomalies, vector, cotangent, taper):
    blocks = lax.axis_size("lat")
    strips = lax.axis_size("lon")
    own = jnp.concatenate([anomalies.reshape(CELLS, LON), vector, cotangent], 0)
    first, second, wide, fields = edge_messages(own, taper)
    swaps = ([], [])
    for s in range(strips):
        for m in range(4):
            here = 4 * s + m
            there = here + 4 if s < strips - 1 else (m + 2) % 4
            swaps[1 - s % 2].extend([(here, there), (there, here)])
    first = lax.ppermute(first, ("lon", "mem"), swaps[0])
    second = lax.ppermute(second, ("lon", "mem"), swaps[1])
    band, rim = bands(wide)
    first, second, band, rim = lax.optimization_barrier((first, second, band, rim))
    message = call(
        message_kernel, shape(PART, LON, dtype=BF16), [], own, first, second
    )
    gathered = lax.all_gather(message, "mem", axis=0, tiled=True)

    down = [(4 * z + m, 4 * z + 4 + m) for z in range(blocks - 1) for m in (0, 1)]
    up = [(4 * z + 4 + m, 4 * z + m) for z in range(blocks - 1) for m in (2, 3)]
    message = lat_message(gathered, fields)
    message, gathered = lax.optimization_barrier((message, gathered))
    lat_halo = lax.ppermute(message, ("lat", "mem"), down + up)
    pushed_out, scaled, corner, wide = rim_push(gathered, fields, band)
    back = lax.ppermute(
        pushed_out.astype(jnp.float16), ("lat", "mem"), [(b, a) for a, b in down + up]
    )
    pushed = block_push(scaled, corner, band)
    keep, send, window, halos = first_sum(
        wide, lat_halo, fields, band, rim, pushed
    )
    back, send = lax.optimization_barrier((back, send))
    back = back.astype(F32)
    send = near_parts(send, back, fields)
    send, window = lax.optimization_barrier((send, window))
    more = lax.ppermute(send, "mem", [(0, 1), (1, 0), (2, 3), (3, 2)])
    early = early_taps(window, halos, fields)
    more, early = lax.optimization_barrier((more, early))
    mine, send = far_parts(keep, more, back, fields)
    half = lax.ppermute(send.astype(jnp.float16), "mem", [(0, 2), (2, 0), (1, 3), (3, 1)])
    mine, early = lax.optimization_barrier((mine, early))
    grad_taper = late_taps(window, halos, fields, early)
    more = half.astype(F32)
    grad_anomalies = mine + more[:CELLS] * jnp.exp2(more[CELLS : CELLS + 1])
    grad_anomalies = grad_anomalies.reshape(GROUP, CLAT, LON)
    return grad_taper, grad_anomalies


def solution(mesh):
    placed = (
        P("mem", "lat", "lon"),
        P("lat", "lon"),
        P("lat", "lon"),
        P(None, ("lat", "mem"), "lon"),
    )
    return jax.shard_map(
        body,
        mesh=mesh,
        in_specs=placed,
        out_specs=(P(None, ("lat", "mem"), "lon"), P("mem", "lat", "lon")),
        check_vma=False,
    )
```

```python
import jax
import jax.numpy as jnp
from jax import lax
from jax.experimental import pallas as pl
from jax.experimental.pallas import tpu as pltpu
from jax.sharding import PartitionSpec as P

SPAN = 17
RIM = 8
TAPS = SPAN * SPAN
ROWS = 4
CLAT = 16
LON = 128
WIN = ROWS + 2 * RIM
RING = CLAT + RIM
GROUP = 20
MEMBERS = 80
DEPTH = 88
CELLS = GROUP * CLAT
EDGES = 64
TAPE = 24
PART = CELLS + 48
HALO = 3 * LON
MAIN = WIN * LON
BACK = MEMBERS * RIM
LATROWS = MEMBERS * RIM + MEMBERS + RIM + 8
TAPE_ROWS = 1184
F32 = jnp.float32
BF16 = jnp.bfloat16
VMEM = pltpu.VMEM
SHARE = 1.0 / (MEMBERS - 1)


def lanes(shape):
    return lax.broadcasted_iota(jnp.int32, shape, len(shape) - 1)


def rows_of(shape):
    return lax.broadcasted_iota(jnp.int32, shape, len(shape) - 2)


def shape(*dims, dtype=F32):
    return jax.ShapeDtypeStruct(dims, dtype)


def call(kernel, out_shape, scratch, *args, limit=16, flops=0):
    return pl.pallas_call(
        kernel,
        out_shape=out_shape,
        in_specs=[pl.BlockSpec(memory_space=VMEM)] * len(args),
        out_specs=jax.tree.map(lambda _: pl.BlockSpec(memory_space=VMEM), out_shape),
        scratch_shapes=scratch,
        compiler_params=pltpu.CompilerParams(vmem_limit_bytes=limit * 2**20),
        cost_estimate=pl.CostEstimate(flops=flops, bytes_accessed=2**20, transcendentals=0),
    )(*args)


def edges_kernel(
    own_ref, taper_ref, first_ref, second_ref, wide, fields, cells
):
    for tap in range(TAPS):
        wide[tap * ROWS : tap * ROWS + ROWS] = taper_ref[tap].astype(F32)
    wide[TAPS * ROWS :] = jnp.zeros((TAPE_ROWS - TAPS * ROWS, LON), F32)
    own = own_ref[...].astype(F32)
    fields[...] = own[CELLS:]
    cells[0 : CELLS + 2 * CLAT] = own
    cells[CELLS + 2 * CLAT :] = jnp.zeros((2 * CLAT, LON), F32)
    lane = lanes((TAPE, LON))
    left = jnp.zeros((TAPE, LON), F32)
    right = jnp.zeros((TAPE, LON), F32)
    for lat in range(CLAT):
        part = cells[pl.ds(lat, TAPE, stride=CLAT), :]
        mine = lane // RIM == lat
        left = jnp.where(mine, pltpu.roll(part, RIM * lat, 1), left)
        right = jnp.where(mine, pltpu.roll(part, (RIM * lat + RIM) % LON, 1), right)
    left_rows = [left]
    right_rows = [right]
    lane = lanes((8, LON))
    row = rows_of((8, LON))
    for block in range(5):
        left = jnp.zeros((8, LON), F32)
        right = jnp.zeros((8, LON), F32)
        for sub in range(4):
            a = block * 4 + sub
            if a >= SPAN:
                continue
            for i in range(ROWS):
                to = sub * 32 + i * RIM
                mine = lane // RIM == to // RIM
                part = wide[pl.ds(a * SPAN * ROWS + i, 8, stride=ROWS), :]
                left = jnp.where(mine, pltpu.roll(part, to, 1), left)
                part = wide[pl.ds((a * SPAN + 9) * ROWS + i, 8, stride=ROWS), :]
                right = jnp.where(mine, pltpu.roll(part, (to + RIM) % LON, 1), right)
        for bit in (1, 2, 4):
            moved = pltpu.roll(left, bit, 0)
            moved = jnp.where(row >= bit, moved, 0.0)
            left = jnp.where((lane & bit) != 0, moved, left)
            moved = pltpu.roll(right, 8 - bit, 0)
            moved = jnp.where(row < 8 - bit, moved, 0.0)
            right = jnp.where(((7 - lane) & bit) != 0, moved, right)
        left_rows.append(left)
        right_rows.append(right)
    left = jnp.concatenate(left_rows, 0)
    right = jnp.concatenate(right_rows, 0)
    odd = lax.axis_index("lon") % 2 == 1
    first_ref[...] = jnp.where(odd, right, left).astype(BF16)
    second_ref[...] = jnp.where(odd, left, right).astype(BF16)


def edge_messages(own, taper):
    return call(
        edges_kernel,
        (
            shape(EDGES, LON, dtype=BF16),
            shape(EDGES, LON, dtype=BF16),
            shape(TAPE_ROWS, LON),
            shape(2 * CLAT, LON),
        ),
        [VMEM(((GROUP + 4) * CLAT, LON), F32)],
        own,
        taper,
    )


def message_kernel(own_ref, first_ref, second_ref, out_ref, edges):
    out_ref[0:CELLS] = own_ref[0:CELLS]
    first = first_ref[...].astype(F32)
    second = second_ref[...].astype(F32)
    odd = lax.axis_index("lon") % 2 == 1
    east = jnp.where(odd, first, second)
    west = jnp.where(odd, second, first)
    edges[0:EDGES] = east
    edges[EDGES:] = west
    halos = [east[0:GROUP], west[0:GROUP], jnp.zeros((8, LON), F32)]
    out_ref[CELLS:] = jnp.concatenate(halos, 0).astype(BF16)


def ring_row(mem, j):
    lat = ROWS * mem - RIM + j
    return jnp.where(lat < 0, lat + RING, lat)


def halo_row(side, ring):
    inside = side * LON + RIM * ring
    outside = 2 * LON + side * (LON // 2) + RIM * (ring - CLAT)
    return jnp.where(ring < CLAT, inside, outside)


def bands_kernel(wide, band_ref, rim_ref, narrow):
    mem = lax.axis_index("mem")
    narrow[...] = jnp.zeros(narrow.shape, F32)
    for i in range(ROWS):
        for j in range(WIN):
            if j < i or j > i + SPAN - 1:
                band_ref[j * LON : (j + 1) * LON, i * LON : (i + 1) * LON] = jnp.zeros(
                    (LON, LON), BF16
                )
    lane = lanes((24, LON))
    row = rows_of((24, LON))
    group = lanes((8, LON)) // 8
    zero = jnp.zeros((8, LON), F32)

    @pl.loop(0, SPAN)
    def _(a):
        for i in range(ROWS):
            taps = wide[pl.ds(a * SPAN * ROWS + i, 24, stride=ROWS), :]
            taps = jnp.where(row < SPAN, taps, 0.0)
            for bit in (1, 2, 4):
                taps = jnp.where((lane & bit) != 0, pltpu.roll(taps, bit, 0), taps)
            low, mid, high = taps[0:8], taps[8:16], taps[16:24]
            parts = []
            for block in range(CLAT):
                part = jnp.where(group == block, mid, zero)
                if block < 15:
                    part = jnp.where(group == block + 1, low, part)
                if block > 0:
                    part = jnp.where(group == block - 1, high, part)
                parts.append(part)
            band_ref[pl.ds(pl.multiple_of((a + i) * LON, LON), LON), i * LON : (i + 1) * LON] = (
                jnp.concatenate(parts, 0).astype(BF16)
            )
            ring = ring_row(mem, a + i)
            east = pl.multiple_of(halo_row(0, ring), 8)
            west = pl.multiple_of(halo_row(1, ring), 8)
            narrow[pl.ds(east, 8), i * LON : (i + 1) * LON] = jnp.where(group == 15, high, zero)
            narrow[pl.ds(west, 8), i * LON : (i + 1) * LON] = jnp.where(group == 0, low, zero)

    rim_ref[...] = narrow[...].astype(BF16)


def bands(wide):
    return call(
        bands_kernel,
        (shape(MAIN, ROWS * LON, dtype=BF16), shape(HALO, ROWS * LON, dtype=BF16)),
        [VMEM((HALO, ROWS * LON), F32)],
        wide,
    )


def split(value):
    high = value.astype(BF16)
    return high, (value - high.astype(F32)).astype(BF16)


def gathered_rows(wide, start, stride):
    parts = [wide[pl.ds(g * PART + start, GROUP, stride=stride), :] for g in range(4)]
    return jnp.concatenate(parts, 0)


def halo_cells(wide, side, pitch=PART):
    parts = []
    for g in range(4):
        at = (g + 1) * pitch - 48 + side * GROUP
        parts.append(wide[at : at + GROUP])
    return jnp.concatenate(parts, 0)


def halo_field(edges, side, which):
    at = side * EDGES + GROUP + which
    return edges[at : at + 1]


def lat_kernel(x_ref, fields, edges, out_ref, halos, rows):
    mem = lax.axis_index("mem")
    upper = mem < 2
    first = jnp.where(upper, RIM, 0)
    for m in range(0, MEMBERS, 2):
        at = (m // GROUP) * PART + (m % GROUP) * CLAT
        pair = x_ref[at : at + 2 * CLAT].astype(F32)
        one = jnp.where(upper, pair[RIM:CLAT], pair[0:RIM])
        two = jnp.where(upper, pair[CLAT + RIM :], pair[CLAT : CLAT + RIM])
        out_ref[m * RIM : m * RIM + CLAT] = jnp.concatenate([one, two], 0).astype(BF16)
    for g in range(4):
        halos[g * 48 : g * 48 + 48] = x_ref[g * PART + CELLS : (g + 1) * PART].astype(F32)
    lane = lanes((MEMBERS + 8, LON))
    pad = jnp.zeros((7, LON), F32)
    sides = []
    for side in range(2):
        cells = [halo_cells(halos, side, 48), halo_field(edges, side, 0), pad]
        sides.append(jnp.concatenate(cells, 0))
    half = LON // 2
    low = jnp.where(lane < half, sides[0], pltpu.roll(sides[1], half, 1))
    high = jnp.where(lane < half, pltpu.roll(sides[0], half, 1), sides[1])
    both = jnp.where(mem < 2, high, low)
    rows[0:MEMBERS] = both[:MEMBERS]
    rows[MEMBERS : MEMBERS + RIM] = fields[pl.ds(pl.multiple_of(first, 8), RIM), :]
    rows[MEMBERS + RIM :] = both[MEMBERS:]
    out_ref[MEMBERS * RIM :] = rows[...].astype(BF16)


def lat_message(gathered, fields, edges):
    return call(
        lat_kernel,
        shape(LATROWS, LON, dtype=BF16),
        [VMEM((4 * 48, LON), F32), VMEM((LATROWS - MEMBERS * RIM, LON), F32)],
        gathered,
        fields,
        edges,
    )


def rim_steps(mem):
    first = jnp.where(mem < 2, 0, jnp.where(mem == 2, 4, 3))
    return first, jnp.where((mem == 0) | (mem == 3), 2, 1)


def block_steps(mem):
    first = jnp.where(mem == 0, 2, jnp.where(mem == 1, 1, 0))
    return first, jnp.where((mem == 0) | (mem == 3), 3, 4)


def pushes(scaled, corner, band_ref, step):
    at = pl.ds(pl.multiple_of(step * STEP * LON, LON), STEP * LON)
    both = lax.dot_general(
        scaled[:, : ROWS * LON],
        band_ref[at, :],
        (((1,), (1,)), ((), ())),
        preferred_element_type=F32,
    )
    both = both + lax.dot_general(
        scaled[:, ROWS * LON :],
        corner[at, :],
        (((1,), (1,)), ((), ())),
        preferred_element_type=F32,
    )
    return both[:MEMBERS] + both[MEMBERS:]


def by_core(mem, members):
    even = jnp.concatenate([members[0:GROUP], members[2 * GROUP : 3 * GROUP]], 0)
    odd = jnp.concatenate([members[GROUP : 2 * GROUP], members[3 * GROUP :]], 0)
    first = mem % 2 == 0
    return jnp.where(first, even, odd), jnp.where(first, odd, even)


def scale_down(ref, rows):
    values = ref[0:rows]
    largest = jnp.full((16, LON), jnp.max(jnp.abs(values)), F32)
    power = jnp.clip(jnp.round(jnp.log2(largest)) - 8.0, -120.0, 100.0)
    ref[0:rows] = values * jnp.exp2(-power)[0:1]
    ref[rows : rows + 16] = power


def rim_push_kernel(x_ref, fields, edges, band_ref, rim_ref, scaled, corner, wide):
    mem = lax.axis_index("mem")
    wide[...] = x_ref[...].astype(F32)
    for i in range(ROWS):
        own = gathered_rows(wide, ROWS * mem + i, CLAT) * fields[pl.ds(CLAT + ROWS * mem + i, 1), :]
        high, low = split(own)
        scaled[0:MEMBERS, i * LON : (i + 1) * LON] = high
        scaled[MEMBERS:, i * LON : (i + 1) * LON] = low
    lane = lanes((MEMBERS, LON))
    east = halo_cells(wide, 0) * halo_field(edges, 0, 1)
    west = halo_cells(wide, 1) * halo_field(edges, 1, 1)
    east = pltpu.roll(east, (LON - 32 * mem) % LON, 1)
    west = pltpu.roll(west, (LON + 32 - 32 * mem) % LON, 1)
    high, low = split(jnp.where(lane < 32, east, jnp.where(lane < 64, west, 0.0)))
    scaled[0:MEMBERS, ROWS * LON :] = high
    scaled[MEMBERS:, ROWS * LON :] = low
    lane = lanes((8, LON))
    corner[...] = jnp.zeros(corner.shape, BF16)
    tiles = []
    for side in range(2):
        packed = edges[side * EDGES + TAPE : (side + 1) * EDGES]
        tiles.append(
            [
                pltpu.roll(
                    packed[8 * (a // 4) : 8 * (a // 4) + 8],
                    (LON + 32 * side - 32 * (a % 4)) % LON,
                    1,
                )
                for a in range(SPAN)
            ]
        )
    zero = jnp.zeros((8, LON), F32)
    for j in range(WIN):
        edge = []
        for side in range(2):
            tile = zero
            for i in range(ROWS):
                if 0 <= j - i < SPAN:
                    tile = jnp.where(lane // RIM == 4 * side + i, tiles[side][j - i], tile)
            edge.append(tile)
        corner[j * LON : j * LON + 16] = jnp.concatenate([edge[1], zero], 0).astype(BF16)
        corner[j * LON + 112 : j * LON + 128] = jnp.concatenate([zero, edge[0]], 0).astype(BF16)
    zeros = jnp.zeros((MEMBERS, LON), F32)

    @pl.when((mem == 1) | (mem == 2))
    def _():
        first = jnp.where(mem == 1, 0, ROWS)
        for k in range(ROWS):
            rim_ref[pl.ds(first + k, MEMBERS, stride=RIM), :] = zeros

    first, steps = rim_steps(mem)

    @pl.loop(first, first + steps)
    def _(step):
        total = pushes(scaled, corner, band_ref, step)
        for k in range(STEP):
            row = pl.ds(ring_row(mem, step * STEP + k) - CLAT, MEMBERS, stride=RIM)
            rim_ref[row, :] = total[:, k * LON : (k + 1) * LON]

    scale_down(rim_ref, BACK)


def block_push_kernel(scaled, corner, band_ref, out_ref):
    mem = lax.axis_index("mem")
    zeros = jnp.zeros((MEMBERS, LON), F32)

    @pl.when((mem == 0) | (mem == 3))
    def _():
        first = jnp.where(mem == 0, CLAT - ROWS, 0)
        for k in range(ROWS):
            out_ref[pl.ds(first + k, MEMBERS, stride=CLAT), :] = zeros

    first, steps = block_steps(mem)

    @pl.loop(first, first + steps)
    def _(step):
        total = pushes(scaled, corner, band_ref, step)
        for k in range(STEP):
            row = ring_row(mem, step * STEP + k)
            out_ref[pl.ds(row, MEMBERS, stride=CLAT), :] = total[:, k * LON : (k + 1) * LON]


STEP = 4


def rim_push(gathered, fields, edges, band):
    return call(
        rim_push_kernel,
        (
            shape(BACK + 16, LON),
            shape(2 * MEMBERS, (ROWS + 1) * LON, dtype=BF16),
            shape(MAIN, LON, dtype=BF16),
            shape(4 * PART, LON),
        ),
        [],
        gathered,
        fields,
        edges,
        band,
        flops=10**6,
    )


def block_push(scaled, corner, band):
    return call(
        block_push_kernel,
        shape(MEMBERS * CLAT, LON),
        [],
        scaled,
        corner,
        band,
        flops=10**6,
    )


def first_kernel(
    wide, lat_ref, fields, edges, band_ref, rim_ref, push_ref,
    keep_ref, send_ref, window, halos,
    wide_lat, scaled,
):
    mem = lax.axis_index("mem")
    wide_lat[...] = lat_ref[...].astype(F32)
    base = MEMBERS * RIM
    pad = jnp.zeros((DEPTH - MEMBERS - 1, LON), F32)
    for j in range(WIN):
        ring = ring_row(mem, j)

        @pl.when(ring < CLAT)
        def _():
            window[j, 0:MEMBERS] = gathered_rows(wide, ring, CLAT)
            window[j, MEMBERS:] = jnp.concatenate([fields[pl.ds(ring, 1), :], pad], 0)

        @pl.when(ring >= CLAT)
        def _():
            window[j, 0:MEMBERS] = wide_lat[pl.ds(ring - CLAT, MEMBERS, stride=RIM), :]
            row = wide_lat[pl.ds(base + MEMBERS + ring - CLAT, 1), :]
            window[j, MEMBERS:] = jnp.concatenate([row, pad], 0)

    for side in range(2):
        halos[side, 0:MEMBERS] = halo_cells(wide, side)
        halos[side, MEMBERS:] = jnp.concatenate([halo_field(edges, side, 0), pad], 0)
    halos[2, 0:MEMBERS] = wide_lat[base : base + MEMBERS]
    last = wide_lat[base + MEMBERS + RIM : base + MEMBERS + RIM + 1]
    halos[2, MEMBERS:] = jnp.concatenate([last, pad], 0)

    def put(at, cells):
        high, low = split(cells[0:MEMBERS] * cells[MEMBERS : MEMBERS + 1])
        scaled[0:MEMBERS, at : at + LON] = high
        scaled[MEMBERS:, at : at + LON] = low

    for j in range(WIN):
        put(j * LON, window[j])
    for k in range(3):
        put(MAIN + k * LON, halos[k])
    both = jnp.dot(scaled[:, :MAIN], band_ref[...], preferred_element_type=F32)
    both = both + jnp.dot(scaled[:, MAIN:], rim_ref[...], preferred_element_type=F32)
    total = both[:MEMBERS] + both[MEMBERS:]
    v_rows = fields[0:CLAT] * SHARE
    core = mem % 2
    for half in range(2):
        for take, target in ((core, keep_ref), (1 - core, send_ref)):
            for m in range(GROUP):
                at = pl.multiple_of((2 * half + take) * CELLS + m * CLAT, 8)
                to = half * CELLS + m * CLAT
                target[to : to + CLAT] = push_ref[pl.ds(at, CLAT), :] * v_rows
    for i in range(ROWS):
        at = pl.ds(ROWS * mem + i, 2 * GROUP, stride=CLAT)
        c_row = fields[pl.ds(CLAT + ROWS * mem + i, 1), :] * SHARE
        keep, send = by_core(mem, total[:, i * LON : (i + 1) * LON] * c_row)
        keep_ref[at, :] = keep_ref[at, :] + keep
        send_ref[at, :] = send_ref[at, :] + send


def first_sum(wide, lat_halo, fields, edges, band, rim, pushed):
    return call(
        first_kernel,
        (
            shape(2 * CELLS, LON),
            shape(2 * CELLS, LON),
            shape(WIN, DEPTH, LON),
            shape(3, DEPTH, LON),
        ),
        [
            VMEM((LATROWS, LON), F32),
            VMEM((2 * MEMBERS, MAIN + HALO), BF16),
        ],
        wide,
        lat_halo,
        fields,
        edges,
        band,
        rim,
        pushed,
        flops=10**6,
    )


def add_back(mem, take, half, at, back_ref, fields, target):
    first = jnp.where(mem < 2, RIM, 0)
    rows = fields[pl.ds(pl.multiple_of(first, 8), RIM), :] * SHARE
    rows = rows * jnp.exp2(back_ref[BACK : BACK + 1])
    start = (2 * half + take) * GROUP * RIM
    for m in range(GROUP):
        source = pl.ds(pl.multiple_of(start + m * RIM, 8), RIM)
        to = pl.ds(pl.multiple_of(at + m * CLAT + first, 8), RIM)
        target[to, :] = target[to, :] + back_ref[source, :] * rows


def near_kernel(part_ref, back_ref, fields, send_ref):
    mem = lax.axis_index("mem")
    send_ref[...] = part_ref[...]
    for half in range(2):
        add_back(mem, 1 - mem % 2, half, half * CELLS, back_ref, fields, send_ref)


def near_parts(part, back, fields):
    return call(near_kernel, shape(2 * CELLS, LON), [], part, back, fields)


def far_kernel(keep_ref, more_ref, back_ref, fields, mine_ref, send_ref):
    mem = lax.axis_index("mem")
    far = mem // 2
    for take, target in ((far, mine_ref), (1 - far, send_ref)):
        at = pl.ds(pl.multiple_of(take * CELLS, 8), CELLS)
        target[0:CELLS] = keep_ref[at, :] + more_ref[at, :]
        add_back(mem, mem % 2, take, 0, back_ref, fields, target)
    scale_down(send_ref, CELLS)


def far_parts(keep, more, back, fields):
    return call(
        far_kernel, (shape(CELLS, LON), shape(CELLS + 16, LON)), [],
        keep, more, back, fields,
    )


def taper_part(window, halos, fields, flat, own, turned, product, shifted, taps_of):
    mem = lax.axis_index("mem")
    used = range(taps_of[0], taps_of[-1] + ROWS)
    for j in used:
        turned[j * LON : (j + 1) * LON, :] = window[j].T.astype(BF16)
    for k in range(3):
        turned[MAIN + k * LON : MAIN + (k + 1) * LON, :] = halos[k].T.astype(BF16)
    keep = rows_of((DEPTH, LON)) < MEMBERS
    for i in range(ROWS):
        own[:, i * LON : (i + 1) * LON] = jnp.where(keep, window[RIM + i], 0.0).astype(BF16)
    own[:, ROWS * LON :] = jnp.where(rows_of((DEPTH, LON)) == MEMBERS, 1.0, 0.0).astype(BF16)
    for j in [*used, WIN, WIN + 1, WIN + 2]:
        at = j * LON
        product[at : at + LON] = jnp.dot(turned[at : at + LON], own[...], preferred_element_type=F32)
    lane = lanes((8, LON))
    wide_lane = lanes((24, LON))

    def diagonals(j, column):
        ring = ring_row(mem, j)
        east = pl.multiple_of(MAIN + halo_row(0, ring), 8)
        west = pl.multiple_of(MAIN + halo_row(1, ring), 8)
        cells = [product[pl.ds(west, 8), column : column + LON]]
        for block in range(CLAT):
            at = pl.multiple_of(j * LON + 8 * block, 8)
            cells.append(product[pl.ds(at, 8), column : column + LON])
        cells.append(product[pl.ds(east, 8), column : column + LON])
        for bit in (8, 4, 2, 1):
            take = (lane & (8 * bit)) != 0
            cells = [jnp.where(take, cells[s + bit], cells[s]) for s in range(len(cells) - bit)]
        taps = jnp.concatenate(cells, 0)
        for bit in (1, 2, 4):
            taps = jnp.where((wide_lane & bit) != 0, pltpu.roll(taps, 24 - bit, 0), taps)
        return taps

    @pl.loop(used[0], used[-1] + 1)
    def _(j):
        shifted[j] = diagonals(j, ROWS * LON)

    @pl.loop(taps_of[0], taps_of[-1] + 1)
    def _(a):
        for i in range(ROWS):
            c_row = fields[pl.ds(CLAT + ROWS * mem + i, 1), :] * SHARE
            taps = diagonals(a + i, i * LON) * shifted[a + i] * c_row
            flat[pl.ds(a * SPAN * ROWS + i, SPAN, stride=ROWS), :] = taps[0:SPAN]


EARLY = 2


def early_kernel(window, halos, fields, flat, *scratch):
    taper_part(window, halos, fields, flat, *scratch, range(EARLY))


def late_kernel(window, halos, fields, early, taper_ref, flat, *scratch):
    taper_part(window, halos, fields, flat, *scratch, range(EARLY, SPAN))
    for tap in range(TAPS):
        source = early if tap < EARLY * SPAN else flat
        taper_ref[tap] = source[tap * ROWS : tap * ROWS + ROWS]


def taper_scratch():
    return [
        VMEM((DEPTH, (ROWS + 1) * LON), BF16),
        VMEM((MAIN + HALO, DEPTH), BF16),
        VMEM((MAIN + HALO, (ROWS + 1) * LON), F32),
        VMEM((WIN, 24, LON), F32),
    ]


def early_taps(window, halos, fields):
    return call(
        early_kernel, shape(EARLY * SPAN * ROWS + 32, LON), taper_scratch(),
        window, halos, fields, limit=24, flops=2 * 10**10,
    )


def late_taps(window, halos, fields, early):
    return call(
        late_kernel, shape(TAPS, ROWS, LON), [VMEM((TAPE_ROWS, LON), F32), *taper_scratch()],
        window, halos, fields, early, limit=24, flops=10**6,
    )


def body(anomalies, vector, cotangent, taper):
    blocks = lax.axis_size("lat")
    strips = lax.axis_size("lon")
    own = jnp.concatenate([anomalies.reshape(CELLS, LON), vector, cotangent], 0)
    first, second, wide, fields = edge_messages(own, taper)
    swaps = ([], [])
    for s in range(strips):
        there = (s + 1) % strips
        swaps[1 - s % 2].extend([(s, there), (there, s)])
    first = lax.ppermute(first, "lon", swaps[0])
    second = lax.ppermute(second, "lon", swaps[1])
    band, rim = bands(wide)
    first, second, band, rim = lax.optimization_barrier((first, second, band, rim))
    message, edges = call(
        message_kernel, (shape(PART, LON, dtype=BF16), shape(2 * EDGES, LON)), [],
        own, first, second,
    )
    gathered = lax.all_gather(message, "mem", axis=0, tiled=True)

    down = [(4 * z + m, 4 * z + 4 + m) for z in range(blocks - 1) for m in (0, 1)]
    up = [(4 * z + 4 + m, 4 * z + m) for z in range(blocks - 1) for m in (2, 3)]
    message = lat_message(gathered, fields, edges)
    message, gathered = lax.optimization_barrier((message, gathered))
    lat_halo = lax.ppermute(message, ("lat", "mem"), down + up)
    pushed_out, scaled, corner, wide = rim_push(gathered, fields, edges, band)
    back = lax.ppermute(
        pushed_out.astype(jnp.float16), ("lat", "mem"), [(b, a) for a, b in down + up]
    )
    pushed = block_push(scaled, corner, band)
    keep, send, window, halos = first_sum(
        wide, lat_halo, fields, edges, band, rim, pushed
    )
    back, send = lax.optimization_barrier((back, send))
    back = back.astype(F32)
    send = near_parts(send, back, fields)
    send, window = lax.optimization_barrier((send, window))
    more = lax.ppermute(send, "mem", [(0, 1), (1, 0), (2, 3), (3, 2)])
    early = early_taps(window, halos, fields)
    more, early = lax.optimization_barrier((more, early))
    mine, send = far_parts(keep, more, back, fields)
    half = lax.ppermute(send.astype(jnp.float16), "mem", [(0, 2), (2, 0), (1, 3), (3, 1)])
    mine, early = lax.optimization_barrier((mine, early))
    grad_taper = late_taps(window, halos, fields, early)
    more = half.astype(F32)
    grad_anomalies = mine + more[:CELLS] * jnp.exp2(more[CELLS : CELLS + 1])
    grad_anomalies = grad_anomalies.reshape(GROUP, CLAT, LON)
    return grad_taper, grad_anomalies


def solution(mesh):
    placed = (
        P("mem", "lat", "lon"),
        P("lat", "lon"),
        P("lat", "lon"),
        P(None, ("lat", "mem"), "lon"),
    )
    return jax.shard_map(
        body,
        mesh=mesh,
        in_specs=placed,
        out_specs=(P(None, ("lat", "mem"), "lon"), P("mem", "lat", "lon")),
        check_vma=False,
    )
```

```python
import jax
import jax.numpy as jnp
from jax import lax
from jax.experimental import pallas as pl
from jax.experimental.pallas import tpu as pltpu
from jax.sharding import PartitionSpec as P

SPAN = 17
RIM = 8
TAPS = SPAN * SPAN
ROWS = 4
CLAT = 16
LON = 128
WIN = ROWS + 2 * RIM
RING = CLAT + RIM
GROUP = 20
MEMBERS = 80
DEPTH = 88
CELLS = GROUP * CLAT
EDGES = 64
TAPE = 24
PART = CELLS + 48
HALO = 3 * LON
MAIN = WIN * LON
BACK = 2 * GROUP * RIM
LATROWS = MEMBERS * RIM + MEMBERS + RIM + 8
TAPE_ROWS = 1184
F32 = jnp.float32
BF16 = jnp.bfloat16
VMEM = pltpu.VMEM
SHARE = 1.0 / (MEMBERS - 1)


def lanes(shape):
    return lax.broadcasted_iota(jnp.int32, shape, len(shape) - 1)


def rows_of(shape):
    return lax.broadcasted_iota(jnp.int32, shape, len(shape) - 2)


def shape(*dims, dtype=F32):
    return jax.ShapeDtypeStruct(dims, dtype)


def call(kernel, out_shape, scratch, *args, limit=16, flops=0):
    return pl.pallas_call(
        kernel,
        out_shape=out_shape,
        in_specs=[pl.BlockSpec(memory_space=VMEM)] * len(args),
        out_specs=jax.tree.map(lambda _: pl.BlockSpec(memory_space=VMEM), out_shape),
        scratch_shapes=scratch,
        compiler_params=pltpu.CompilerParams(vmem_limit_bytes=limit * 2**20),
        cost_estimate=pl.CostEstimate(flops=flops, bytes_accessed=2**20, transcendentals=0),
    )(*args)


def edges_kernel(
    own_ref, taper_ref, first_ref, second_ref, wide, fields, cells
):
    for tap in range(TAPS):
        wide[tap * ROWS : tap * ROWS + ROWS] = taper_ref[tap].astype(F32)
    wide[TAPS * ROWS :] = jnp.zeros((TAPE_ROWS - TAPS * ROWS, LON), F32)
    own = own_ref[...].astype(F32)
    fields[...] = own[CELLS:]
    cells[0 : CELLS + 2 * CLAT] = own
    cells[CELLS + 2 * CLAT :] = jnp.zeros((2 * CLAT, LON), F32)
    lane = lanes((TAPE, LON))
    left = jnp.zeros((TAPE, LON), F32)
    right = jnp.zeros((TAPE, LON), F32)
    for lat in range(CLAT):
        part = cells[pl.ds(lat, TAPE, stride=CLAT), :]
        mine = lane // RIM == lat
        left = jnp.where(mine, pltpu.roll(part, RIM * lat, 1), left)
        right = jnp.where(mine, pltpu.roll(part, (RIM * lat + RIM) % LON, 1), right)
    left_rows = [left]
    right_rows = [right]
    lane = lanes((8, LON))
    row = rows_of((8, LON))
    for block in range(5):
        left = jnp.zeros((8, LON), F32)
        right = jnp.zeros((8, LON), F32)
        for sub in range(4):
            a = block * 4 + sub
            if a >= SPAN:
                continue
            for i in range(ROWS):
                to = sub * 32 + i * RIM
                mine = lane // RIM == to // RIM
                part = wide[pl.ds(a * SPAN * ROWS + i, 8, stride=ROWS), :]
                left = jnp.where(mine, pltpu.roll(part, to, 1), left)
                part = wide[pl.ds((a * SPAN + 9) * ROWS + i, 8, stride=ROWS), :]
                right = jnp.where(mine, pltpu.roll(part, (to + RIM) % LON, 1), right)
        for bit in (1, 2, 4):
            moved = pltpu.roll(left, bit, 0)
            moved = jnp.where(row >= bit, moved, 0.0)
            left = jnp.where((lane & bit) != 0, moved, left)
            moved = pltpu.roll(right, 8 - bit, 0)
            moved = jnp.where(row < 8 - bit, moved, 0.0)
            right = jnp.where(((7 - lane) & bit) != 0, moved, right)
        left_rows.append(left)
        right_rows.append(right)
    left = jnp.concatenate(left_rows, 0)
    right = jnp.concatenate(right_rows, 0)
    odd = lax.axis_index("lon") % 2 == 1
    first_ref[...] = jnp.where(odd, right, left).astype(BF16)
    second_ref[...] = jnp.where(odd, left, right).astype(BF16)


def edge_messages(own, taper):
    return call(
        edges_kernel,
        (
            shape(EDGES, LON, dtype=BF16),
            shape(EDGES, LON, dtype=BF16),
            shape(TAPE_ROWS, LON),
            shape(2 * CLAT, LON),
        ),
        [VMEM(((GROUP + 4) * CLAT, LON), F32)],
        own,
        taper,
    )


def message_kernel(own_ref, first_ref, second_ref, out_ref, edges):
    out_ref[0:CELLS] = own_ref[0:CELLS]
    first = first_ref[...].astype(F32)
    second = second_ref[...].astype(F32)
    odd = lax.axis_index("lon") % 2 == 1
    east = jnp.where(odd, first, second)
    west = jnp.where(odd, second, first)
    edges[0:EDGES] = east
    edges[EDGES:] = west
    halos = [east[0:GROUP], west[0:GROUP], jnp.zeros((8, LON), F32)]
    out_ref[CELLS:] = jnp.concatenate(halos, 0).astype(BF16)


def ring_row(mem, j):
    lat = ROWS * mem - RIM + j
    return jnp.where(lat < 0, lat + RING, lat)


def halo_row(side, ring):
    inside = side * LON + RIM * ring
    outside = 2 * LON + side * (LON // 2) + RIM * (ring - CLAT)
    return jnp.where(ring < CLAT, inside, outside)


def bands_kernel(wide, band_ref, rim_ref, narrow):
    mem = lax.axis_index("mem")
    narrow[...] = jnp.zeros(narrow.shape, F32)
    for i in range(ROWS):
        for j in range(WIN):
            if j < i or j > i + SPAN - 1:
                band_ref[j * LON : (j + 1) * LON, i * LON : (i + 1) * LON] = jnp.zeros(
                    (LON, LON), BF16
                )
    lane = lanes((24, LON))
    row = rows_of((24, LON))
    group = lanes((8, LON)) // 8
    zero = jnp.zeros((8, LON), F32)

    @pl.loop(0, SPAN)
    def _(a):
        for i in range(ROWS):
            taps = wide[pl.ds(a * SPAN * ROWS + i, 24, stride=ROWS), :]
            taps = jnp.where(row < SPAN, taps, 0.0)
            for bit in (1, 2, 4):
                taps = jnp.where((lane & bit) != 0, pltpu.roll(taps, bit, 0), taps)
            low, mid, high = taps[0:8], taps[8:16], taps[16:24]
            parts = []
            for block in range(CLAT):
                part = jnp.where(group == block, mid, zero)
                if block < 15:
                    part = jnp.where(group == block + 1, low, part)
                if block > 0:
                    part = jnp.where(group == block - 1, high, part)
                parts.append(part)
            band_ref[pl.ds(pl.multiple_of((a + i) * LON, LON), LON), i * LON : (i + 1) * LON] = (
                jnp.concatenate(parts, 0).astype(BF16)
            )
            ring = ring_row(mem, a + i)
            east = pl.multiple_of(halo_row(0, ring), 8)
            west = pl.multiple_of(halo_row(1, ring), 8)
            narrow[pl.ds(east, 8), i * LON : (i + 1) * LON] = jnp.where(group == 15, high, zero)
            narrow[pl.ds(west, 8), i * LON : (i + 1) * LON] = jnp.where(group == 0, low, zero)

    rim_ref[...] = narrow[...].astype(BF16)


def bands(wide):
    return call(
        bands_kernel,
        (shape(MAIN, ROWS * LON, dtype=BF16), shape(HALO, ROWS * LON, dtype=BF16)),
        [VMEM((HALO, ROWS * LON), F32)],
        wide,
    )


def split(value):
    high = value.astype(BF16)
    return high, (value - high.astype(F32)).astype(BF16)


def gathered_rows(wide, start, stride):
    parts = [wide[pl.ds(g * PART + start, GROUP, stride=stride), :] for g in range(4)]
    return jnp.concatenate(parts, 0)


def halo_cells(wide, side, pitch=PART):
    parts = []
    for g in range(4):
        at = (g + 1) * pitch - 48 + side * GROUP
        parts.append(wide[at : at + GROUP])
    return jnp.concatenate(parts, 0)


def halo_field(edges, side, which):
    at = side * EDGES + GROUP + which
    return edges[at : at + 1]


def lat_kernel(x_ref, fields, edges, out_ref, halos, rows):
    mem = lax.axis_index("mem")
    upper = mem < 2
    first = jnp.where(upper, RIM, 0)
    for m in range(0, MEMBERS, 2):
        at = (m // GROUP) * PART + (m % GROUP) * CLAT
        pair = x_ref[at : at + 2 * CLAT].astype(F32)
        one = jnp.where(upper, pair[RIM:CLAT], pair[0:RIM])
        two = jnp.where(upper, pair[CLAT + RIM :], pair[CLAT : CLAT + RIM])
        out_ref[m * RIM : m * RIM + CLAT] = jnp.concatenate([one, two], 0).astype(BF16)
    for g in range(4):
        halos[g * 48 : g * 48 + 48] = x_ref[g * PART + CELLS : (g + 1) * PART].astype(F32)
    lane = lanes((MEMBERS + 8, LON))
    pad = jnp.zeros((7, LON), F32)
    sides = []
    for side in range(2):
        cells = [halo_cells(halos, side, 48), halo_field(edges, side, 0), pad]
        sides.append(jnp.concatenate(cells, 0))
    half = LON // 2
    low = jnp.where(lane < half, sides[0], pltpu.roll(sides[1], half, 1))
    high = jnp.where(lane < half, pltpu.roll(sides[0], half, 1), sides[1])
    both = jnp.where(mem < 2, high, low)
    rows[0:MEMBERS] = both[:MEMBERS]
    rows[MEMBERS : MEMBERS + RIM] = fields[pl.ds(pl.multiple_of(first, 8), RIM), :]
    rows[MEMBERS + RIM :] = both[MEMBERS:]
    out_ref[MEMBERS * RIM :] = rows[...].astype(BF16)


def lat_message(gathered, fields, edges):
    return call(
        lat_kernel,
        shape(LATROWS, LON, dtype=BF16),
        [VMEM((4 * 48, LON), F32), VMEM((LATROWS - MEMBERS * RIM, LON), F32)],
        gathered,
        fields,
        edges,
    )


def rim_steps(mem):
    first = jnp.where(mem < 2, 0, jnp.where(mem == 2, 4, 3))
    return first, jnp.where((mem == 0) | (mem == 3), 2, 1)


def block_steps(mem):
    first = jnp.where(mem == 0, 2, jnp.where(mem == 1, 1, 0))
    return first, jnp.where((mem == 0) | (mem == 3), 3, 4)


def pushes(scaled, corner, band_ref, step):
    at = pl.ds(pl.multiple_of(step * STEP * LON, LON), STEP * LON)
    both = lax.dot_general(
        scaled[:, : ROWS * LON],
        band_ref[at, :],
        (((1,), (1,)), ((), ())),
        preferred_element_type=F32,
    )
    both = both + lax.dot_general(
        scaled[:, ROWS * LON :],
        corner[at, :],
        (((1,), (1,)), ((), ())),
        preferred_element_type=F32,
    )
    return both[:MEMBERS] + both[MEMBERS:]


def by_core(mem, members):
    even = jnp.concatenate([members[0:GROUP], members[2 * GROUP : 3 * GROUP]], 0)
    odd = jnp.concatenate([members[GROUP : 2 * GROUP], members[3 * GROUP :]], 0)
    first = mem % 2 == 0
    return jnp.where(first, even, odd), jnp.where(first, odd, even)


def scale_down(ref, rows):
    values = ref[0:rows]
    largest = jnp.full((16, LON), jnp.max(jnp.abs(values)), F32)
    power = jnp.clip(jnp.round(jnp.log2(largest)) - 8.0, -120.0, 100.0)
    ref[0:rows] = values * jnp.exp2(-power)[0:1]
    ref[rows : rows + 16] = power


def rim_push_kernel(
    x_ref, fields, edges, band_ref, near_ref, cross_ref, scaled, corner, wide
):
    mem = lax.axis_index("mem")
    wide[...] = x_ref[...].astype(F32)
    for i in range(ROWS):
        own = gathered_rows(wide, ROWS * mem + i, CLAT) * fields[pl.ds(CLAT + ROWS * mem + i, 1), :]
        high, low = split(own)
        scaled[0:MEMBERS, i * LON : (i + 1) * LON] = high
        scaled[MEMBERS:, i * LON : (i + 1) * LON] = low
    lane = lanes((MEMBERS, LON))
    east = halo_cells(wide, 0) * halo_field(edges, 0, 1)
    west = halo_cells(wide, 1) * halo_field(edges, 1, 1)
    east = pltpu.roll(east, (LON - 32 * mem) % LON, 1)
    west = pltpu.roll(west, (LON + 32 - 32 * mem) % LON, 1)
    high, low = split(jnp.where(lane < 32, east, jnp.where(lane < 64, west, 0.0)))
    scaled[0:MEMBERS, ROWS * LON :] = high
    scaled[MEMBERS:, ROWS * LON :] = low
    lane = lanes((8, LON))
    corner[...] = jnp.zeros(corner.shape, BF16)
    tiles = []
    for side in range(2):
        packed = edges[side * EDGES + TAPE : (side + 1) * EDGES]
        tiles.append(
            [
                pltpu.roll(
                    packed[8 * (a // 4) : 8 * (a // 4) + 8],
                    (LON + 32 * side - 32 * (a % 4)) % LON,
                    1,
                )
                for a in range(SPAN)
            ]
        )
    zero = jnp.zeros((8, LON), F32)
    for j in range(WIN):
        edge = []
        for side in range(2):
            tile = zero
            for i in range(ROWS):
                if 0 <= j - i < SPAN:
                    tile = jnp.where(lane // RIM == 4 * side + i, tiles[side][j - i], tile)
            edge.append(tile)
        corner[j * LON : j * LON + 16] = jnp.concatenate([edge[1], zero], 0).astype(BF16)
        corner[j * LON + 112 : j * LON + 128] = jnp.concatenate([zero, edge[0]], 0).astype(BF16)
    zeros = jnp.zeros((2 * GROUP, LON), F32)

    @pl.when((mem == 1) | (mem == 2))
    def _():
        first = jnp.where(mem == 1, 0, ROWS)
        for k in range(ROWS):
            near_ref[pl.ds(first + k, 2 * GROUP, stride=RIM), :] = zeros
            cross_ref[pl.ds(first + k, 2 * GROUP, stride=RIM), :] = zeros

    first, steps = rim_steps(mem)

    @pl.loop(first, first + steps)
    def _(step):
        near, cross = by_core(mem, pushes(scaled, corner, band_ref, step))
        for k in range(STEP):
            row = pl.ds(ring_row(mem, step * STEP + k) - CLAT, 2 * GROUP, stride=RIM)
            near_ref[row, :] = near[:, k * LON : (k + 1) * LON]
            cross_ref[row, :] = cross[:, k * LON : (k + 1) * LON]

    scale_down(near_ref, BACK)
    scale_down(cross_ref, BACK)


def block_push_kernel(scaled, corner, band_ref, out_ref):
    mem = lax.axis_index("mem")
    zeros = jnp.zeros((MEMBERS, LON), F32)

    @pl.when((mem == 0) | (mem == 3))
    def _():
        first = jnp.where(mem == 0, CLAT - ROWS, 0)
        for k in range(ROWS):
            out_ref[pl.ds(first + k, MEMBERS, stride=CLAT), :] = zeros

    first, steps = block_steps(mem)

    @pl.loop(first, first + steps)
    def _(step):
        total = pushes(scaled, corner, band_ref, step)
        for k in range(STEP):
            row = ring_row(mem, step * STEP + k)
            out_ref[pl.ds(row, MEMBERS, stride=CLAT), :] = total[:, k * LON : (k + 1) * LON]


STEP = 4


def rim_push(gathered, fields, edges, band):
    return call(
        rim_push_kernel,
        (
            shape(BACK + 16, LON),
            shape(BACK + 16, LON),
            shape(2 * MEMBERS, (ROWS + 1) * LON, dtype=BF16),
            shape(MAIN, LON, dtype=BF16),
            shape(4 * PART, LON),
        ),
        [],
        gathered,
        fields,
        edges,
        band,
        flops=10**6,
    )


def block_push(scaled, corner, band):
    return call(
        block_push_kernel,
        shape(MEMBERS * CLAT, LON),
        [],
        scaled,
        corner,
        band,
        flops=10**6,
    )


def first_kernel(
    wide, lat_ref, fields, edges, band_ref, rim_ref, push_ref,
    keep_ref, send_ref, window, halos,
    wide_lat, scaled,
):
    mem = lax.axis_index("mem")
    wide_lat[...] = lat_ref[...].astype(F32)
    base = MEMBERS * RIM
    pad = jnp.zeros((DEPTH - MEMBERS - 1, LON), F32)
    for j in range(WIN):
        ring = ring_row(mem, j)

        @pl.when(ring < CLAT)
        def _():
            window[j, 0:MEMBERS] = gathered_rows(wide, ring, CLAT)
            window[j, MEMBERS:] = jnp.concatenate([fields[pl.ds(ring, 1), :], pad], 0)

        @pl.when(ring >= CLAT)
        def _():
            window[j, 0:MEMBERS] = wide_lat[pl.ds(ring - CLAT, MEMBERS, stride=RIM), :]
            row = wide_lat[pl.ds(base + MEMBERS + ring - CLAT, 1), :]
            window[j, MEMBERS:] = jnp.concatenate([row, pad], 0)

    for side in range(2):
        halos[side, 0:MEMBERS] = halo_cells(wide, side)
        halos[side, MEMBERS:] = jnp.concatenate([halo_field(edges, side, 0), pad], 0)
    halos[2, 0:MEMBERS] = wide_lat[base : base + MEMBERS]
    last = wide_lat[base + MEMBERS + RIM : base + MEMBERS + RIM + 1]
    halos[2, MEMBERS:] = jnp.concatenate([last, pad], 0)

    def put(at, cells):
        high, low = split(cells[0:MEMBERS] * cells[MEMBERS : MEMBERS + 1])
        scaled[0:MEMBERS, at : at + LON] = high
        scaled[MEMBERS:, at : at + LON] = low

    for j in range(WIN):
        put(j * LON, window[j])
    for k in range(3):
        put(MAIN + k * LON, halos[k])
    both = jnp.dot(scaled[:, :MAIN], band_ref[...], preferred_element_type=F32)
    both = both + jnp.dot(scaled[:, MAIN:], rim_ref[...], preferred_element_type=F32)
    total = both[:MEMBERS] + both[MEMBERS:]
    v_rows = fields[0:CLAT] * SHARE
    core = mem % 2
    for half in range(2):
        for take, target in ((core, keep_ref), (1 - core, send_ref)):
            for m in range(GROUP):
                at = pl.multiple_of((2 * half + take) * CELLS + m * CLAT, 8)
                to = half * CELLS + m * CLAT
                target[to : to + CLAT] = push_ref[pl.ds(at, CLAT), :] * v_rows
    for i in range(ROWS):
        at = pl.ds(ROWS * mem + i, 2 * GROUP, stride=CLAT)
        c_row = fields[pl.ds(CLAT + ROWS * mem + i, 1), :] * SHARE
        keep, send = by_core(mem, total[:, i * LON : (i + 1) * LON] * c_row)
        keep_ref[at, :] = keep_ref[at, :] + keep
        send_ref[at, :] = send_ref[at, :] + send


def first_sum(wide, lat_halo, fields, edges, band, rim, pushed):
    return call(
        first_kernel,
        (
            shape(2 * CELLS, LON),
            shape(2 * CELLS, LON),
            shape(WIN, DEPTH, LON),
            shape(3, DEPTH, LON),
        ),
        [
            VMEM((LATROWS, LON), F32),
            VMEM((2 * MEMBERS, MAIN + HALO), BF16),
        ],
        wide,
        lat_halo,
        fields,
        edges,
        band,
        rim,
        pushed,
        flops=10**6,
    )


def merge_kernel(near_ref, cross_ref, fields, out_ref):
    first = jnp.where(lax.axis_index("mem") < 2, RIM, 0)
    rows = fields[pl.ds(pl.multiple_of(first, 8), RIM), :] * SHARE
    near = rows * jnp.exp2(near_ref[BACK : BACK + 1])
    cross = rows * jnp.exp2(cross_ref[BACK : BACK + 1])
    for at in range(0, BACK, RIM):
        out_ref[at : at + RIM] = (
            near_ref[at : at + RIM] * near + cross_ref[at : at + RIM] * cross
        )


def merged(near, cross, fields):
    return call(merge_kernel, shape(BACK, LON), [], near, cross, fields, flops=29 * 10**8)


def far_kernel(keep_ref, more_ref, back_ref, mine_ref, send_ref):
    mem = lax.axis_index("mem")
    far = mem // 2
    first = jnp.where(mem < 2, RIM, 0)
    for take, target in ((far, mine_ref), (1 - far, send_ref)):
        at = pl.ds(pl.multiple_of(take * CELLS, 8), CELLS)
        target[0:CELLS] = keep_ref[at, :] + more_ref[at, :]
        for m in range(GROUP):
            source = pl.ds(pl.multiple_of(take * GROUP * RIM + m * RIM, 8), RIM)
            to = pl.ds(pl.multiple_of(m * CLAT + first, 8), RIM)
            target[to, :] = target[to, :] + back_ref[source, :]
    scale_down(send_ref, CELLS)


def far_parts(keep, more, back):
    return call(
        far_kernel, (shape(CELLS, LON), shape(CELLS + 16, LON)), [], keep, more, back
    )


def taper_part(window, halos, fields, flat, own, turned, product, shifted, taps_of):
    mem = lax.axis_index("mem")
    used = range(taps_of[0], taps_of[-1] + ROWS)
    for j in used:
        turned[j * LON : (j + 1) * LON, :] = window[j].T.astype(BF16)
    for k in range(3):
        turned[MAIN + k * LON : MAIN + (k + 1) * LON, :] = halos[k].T.astype(BF16)
    keep = rows_of((DEPTH, LON)) < MEMBERS
    for i in range(ROWS):
        own[:, i * LON : (i + 1) * LON] = jnp.where(keep, window[RIM + i], 0.0).astype(BF16)
    own[:, ROWS * LON :] = jnp.where(rows_of((DEPTH, LON)) == MEMBERS, 1.0, 0.0).astype(BF16)
    for j in [*used, WIN, WIN + 1, WIN + 2]:
        at = j * LON
        product[at : at + LON] = jnp.dot(turned[at : at + LON], own[...], preferred_element_type=F32)
    lane = lanes((8, LON))
    wide_lane = lanes((24, LON))

    def diagonals(j, column):
        ring = ring_row(mem, j)
        east = pl.multiple_of(MAIN + halo_row(0, ring), 8)
        west = pl.multiple_of(MAIN + halo_row(1, ring), 8)
        cells = [product[pl.ds(west, 8), column : column + LON]]
        for block in range(CLAT):
            at = pl.multiple_of(j * LON + 8 * block, 8)
            cells.append(product[pl.ds(at, 8), column : column + LON])
        cells.append(product[pl.ds(east, 8), column : column + LON])
        for bit in (8, 4, 2, 1):
            take = (lane & (8 * bit)) != 0
            cells = [jnp.where(take, cells[s + bit], cells[s]) for s in range(len(cells) - bit)]
        taps = jnp.concatenate(cells, 0)
        for bit in (1, 2, 4):
            taps = jnp.where((wide_lane & bit) != 0, pltpu.roll(taps, 24 - bit, 0), taps)
        return taps

    @pl.loop(used[0], used[-1] + 1)
    def _(j):
        shifted[j] = diagonals(j, ROWS * LON)

    @pl.loop(taps_of[0], taps_of[-1] + 1)
    def _(a):
        for i in range(ROWS):
            c_row = fields[pl.ds(CLAT + ROWS * mem + i, 1), :] * SHARE
            taps = diagonals(a + i, i * LON) * shifted[a + i] * c_row
            flat[pl.ds(a * SPAN * ROWS + i, SPAN, stride=ROWS), :] = taps[0:SPAN]


EARLY = 2


def early_kernel(window, halos, fields, flat, *scratch):
    taper_part(window, halos, fields, flat, *scratch, range(EARLY))


def late_kernel(window, halos, fields, early, taper_ref, flat, *scratch):
    taper_part(window, halos, fields, flat, *scratch, range(EARLY, SPAN))
    for tap in range(TAPS):
        source = early if tap < EARLY * SPAN else flat
        taper_ref[tap] = source[tap * ROWS : tap * ROWS + ROWS]


def taper_scratch():
    return [
        VMEM((DEPTH, (ROWS + 1) * LON), BF16),
        VMEM((MAIN + HALO, DEPTH), BF16),
        VMEM((MAIN + HALO, (ROWS + 1) * LON), F32),
        VMEM((WIN, 24, LON), F32),
    ]


def early_taps(window, halos, fields):
    return call(
        early_kernel, shape(EARLY * SPAN * ROWS + 32, LON), taper_scratch(),
        window, halos, fields, limit=24, flops=10**6,
    )


def late_taps(window, halos, fields, early):
    return call(
        late_kernel, shape(TAPS, ROWS, LON), [VMEM((TAPE_ROWS, LON), F32), *taper_scratch()],
        window, halos, fields, early, limit=24, flops=10**6,
    )


def body(anomalies, vector, cotangent, taper):
    blocks = lax.axis_size("lat")
    strips = lax.axis_size("lon")
    own = jnp.concatenate([anomalies.reshape(CELLS, LON), vector, cotangent], 0)
    first, second, wide, fields = edge_messages(own, taper)
    swaps = ([], [])
    for s in range(strips):
        there = (s + 1) % strips
        swaps[1 - s % 2].extend([(s, there), (there, s)])
    first = lax.ppermute(first, "lon", swaps[0])
    second = lax.ppermute(second, "lon", swaps[1])
    band, rim = bands(wide)
    first, second, band, rim = lax.optimization_barrier((first, second, band, rim))
    message, edges = call(
        message_kernel, (shape(PART, LON, dtype=BF16), shape(2 * EDGES, LON)), [],
        own, first, second,
    )
    gathered = lax.all_gather(message, "mem", axis=0, tiled=True)

    down = [(4 * z + m, 4 * z + 4 + m) for z in range(blocks - 1) for m in (0, 1)]
    up = [(4 * z + 4 + m, 4 * z + m) for z in range(blocks - 1) for m in (2, 3)]
    message = lat_message(gathered, fields, edges)
    message, gathered = lax.optimization_barrier((message, gathered))
    lat_halo = lax.ppermute(message, ("lat", "mem"), down + up)
    near, cross, scaled, corner, wide = rim_push(gathered, fields, edges, band)
    half = jnp.float16
    near = lax.ppermute(near.astype(half), ("lat", "mem"), [(b, a) for a, b in down + up])
    cross = lax.ppermute(cross.astype(half), ("lat", "mem"), [(b, a ^ 1) for a, b in down + up])
    pushed = block_push(scaled, corner, band)
    keep, send, window, halos = first_sum(
        wide, lat_halo, fields, edges, band, rim, pushed
    )
    more = lax.ppermute(send, "mem", [(0, 1), (1, 0), (2, 3), (3, 2)])
    early = early_taps(window, halos, fields)
    near, cross, early = lax.optimization_barrier((near, cross, early))
    back = merged(near.astype(F32), cross.astype(F32), fields)
    more, early = lax.optimization_barrier((more, early))
    mine, send = far_parts(keep, more, back)
    half = lax.ppermute(send.astype(jnp.float16), "mem", [(0, 2), (2, 0), (1, 3), (3, 1)])
    mine, early = lax.optimization_barrier((mine, early))
    grad_taper = late_taps(window, halos, fields, early)
    more = half.astype(F32)
    grad_anomalies = mine + more[:CELLS] * jnp.exp2(more[CELLS : CELLS + 1])
    grad_anomalies = grad_anomalies.reshape(GROUP, CLAT, LON)
    return grad_taper, grad_anomalies


def solution(mesh):
    placed = (
        P("mem", "lat", "lon"),
        P("lat", "lon"),
        P("lat", "lon"),
        P(None, ("lat", "mem"), "lon"),
    )
    return jax.shard_map(
        body,
        mesh=mesh,
        in_specs=placed,
        out_specs=(P(None, ("lat", "mem"), "lon"), P("mem", "lat", "lon")),
        check_vma=False,
    )
```

```python
import jax
import jax.numpy as jnp
from jax import lax
from jax.experimental import pallas as pl
from jax.experimental.pallas import tpu as pltpu
from jax.sharding import PartitionSpec as P

SPAN = 17
RIM = 8
TAPS = SPAN * SPAN
ROWS = 4
CLAT = 16
LON = 128
WIN = ROWS + 2 * RIM
RING = CLAT + RIM
GROUP = 20
MEMBERS = 80
DEPTH = 88
CELLS = GROUP * CLAT
EDGES = 64
TAPE = 24
PART = CELLS + 48
HALO = 3 * LON
MAIN = WIN * LON
BACK = MEMBERS * RIM
LATROWS = MEMBERS * RIM + MEMBERS + RIM + 8
TAPE_ROWS = 1184
F32 = jnp.float32
BF16 = jnp.bfloat16
VMEM = pltpu.VMEM
SHARE = 1.0 / (MEMBERS - 1)


def lanes(shape):
    return lax.broadcasted_iota(jnp.int32, shape, len(shape) - 1)


def rows_of(shape):
    return lax.broadcasted_iota(jnp.int32, shape, len(shape) - 2)


def shape(*dims, dtype=F32):
    return jax.ShapeDtypeStruct(dims, dtype)


def call(kernel, out_shape, scratch, *args, limit=16, flops=0):
    return pl.pallas_call(
        kernel,
        out_shape=out_shape,
        in_specs=[pl.BlockSpec(memory_space=VMEM)] * len(args),
        out_specs=jax.tree.map(lambda _: pl.BlockSpec(memory_space=VMEM), out_shape),
        scratch_shapes=scratch,
        compiler_params=pltpu.CompilerParams(vmem_limit_bytes=limit * 2**20),
        cost_estimate=pl.CostEstimate(flops=flops, bytes_accessed=2**20, transcendentals=0),
    )(*args)


def edges_kernel(
    own_ref, taper_ref, first_ref, second_ref, wide, fields, cells
):
    for tap in range(TAPS):
        wide[tap * ROWS : tap * ROWS + ROWS] = taper_ref[tap].astype(F32)
    wide[TAPS * ROWS :] = jnp.zeros((TAPE_ROWS - TAPS * ROWS, LON), F32)
    own = own_ref[...].astype(F32)
    fields[...] = own[CELLS:]
    cells[0 : CELLS + 2 * CLAT] = own
    cells[CELLS + 2 * CLAT :] = jnp.zeros((2 * CLAT, LON), F32)
    lane = lanes((TAPE, LON))
    left = jnp.zeros((TAPE, LON), F32)
    right = jnp.zeros((TAPE, LON), F32)
    for lat in range(CLAT):
        part = cells[pl.ds(lat, TAPE, stride=CLAT), :]
        mine = lane // RIM == lat
        left = jnp.where(mine, pltpu.roll(part, RIM * lat, 1), left)
        right = jnp.where(mine, pltpu.roll(part, (RIM * lat + RIM) % LON, 1), right)
    left_rows = [left]
    right_rows = [right]
    lane = lanes((8, LON))
    row = rows_of((8, LON))
    for block in range(5):
        left = jnp.zeros((8, LON), F32)
        right = jnp.zeros((8, LON), F32)
        for sub in range(4):
            a = block * 4 + sub
            if a >= SPAN:
                continue
            for i in range(ROWS):
                to = sub * 32 + i * RIM
                mine = lane // RIM == to // RIM
                part = wide[pl.ds(a * SPAN * ROWS + i, 8, stride=ROWS), :]
                left = jnp.where(mine, pltpu.roll(part, to, 1), left)
                part = wide[pl.ds((a * SPAN + 9) * ROWS + i, 8, stride=ROWS), :]
                right = jnp.where(mine, pltpu.roll(part, (to + RIM) % LON, 1), right)
        for bit in (1, 2, 4):
            moved = pltpu.roll(left, bit, 0)
            moved = jnp.where(row >= bit, moved, 0.0)
            left = jnp.where((lane & bit) != 0, moved, left)
            moved = pltpu.roll(right, 8 - bit, 0)
            moved = jnp.where(row < 8 - bit, moved, 0.0)
            right = jnp.where(((7 - lane) & bit) != 0, moved, right)
        left_rows.append(left)
        right_rows.append(right)
    left = jnp.concatenate(left_rows, 0)
    right = jnp.concatenate(right_rows, 0)
    odd = lax.axis_index("lon") % 2 == 1
    first_ref[...] = jnp.where(odd, right, left).astype(BF16)
    second_ref[...] = jnp.where(odd, left, right).astype(BF16)


def edge_messages(own, taper):
    return call(
        edges_kernel,
        (
            shape(EDGES, LON, dtype=BF16),
            shape(EDGES, LON, dtype=BF16),
            shape(TAPE_ROWS, LON),
            shape(2 * CLAT, LON),
        ),
        [VMEM(((GROUP + 4) * CLAT, LON), F32)],
        own,
        taper,
    )


def message_kernel(own_ref, first_ref, second_ref, out_ref, edges):
    out_ref[0:CELLS] = own_ref[0:CELLS]
    first = first_ref[...].astype(F32)
    second = second_ref[...].astype(F32)
    odd = lax.axis_index("lon") % 2 == 1
    east = jnp.where(odd, first, second)
    west = jnp.where(odd, second, first)
    edges[0:EDGES] = east
    edges[EDGES:] = west
    halos = [east[0:GROUP], west[0:GROUP], jnp.zeros((8, LON), F32)]
    out_ref[CELLS:] = jnp.concatenate(halos, 0).astype(BF16)


def ring_row(mem, j):
    lat = ROWS * mem - RIM + j
    return jnp.where(lat < 0, lat + RING, lat)


def halo_row(side, ring):
    inside = side * LON + RIM * ring
    outside = 2 * LON + side * (LON // 2) + RIM * (ring - CLAT)
    return jnp.where(ring < CLAT, inside, outside)


def bands_kernel(wide, band_ref, rim_ref, narrow):
    mem = lax.axis_index("mem")
    narrow[...] = jnp.zeros(narrow.shape, F32)
    for i in range(ROWS):
        for j in range(WIN):
            if j < i or j > i + SPAN - 1:
                band_ref[j * LON : (j + 1) * LON, i * LON : (i + 1) * LON] = jnp.zeros(
                    (LON, LON), BF16
                )
    lane = lanes((24, LON))
    row = rows_of((24, LON))
    group = lanes((8, LON)) // 8
    zero = jnp.zeros((8, LON), F32)

    @pl.loop(0, SPAN)
    def _(a):
        for i in range(ROWS):
            taps = wide[pl.ds(a * SPAN * ROWS + i, 24, stride=ROWS), :]
            taps = jnp.where(row < SPAN, taps, 0.0)
            for bit in (1, 2, 4):
                taps = jnp.where((lane & bit) != 0, pltpu.roll(taps, bit, 0), taps)
            low, mid, high = taps[0:8], taps[8:16], taps[16:24]
            parts = []
            for block in range(CLAT):
                part = jnp.where(group == block, mid, zero)
                if block < 15:
                    part = jnp.where(group == block + 1, low, part)
                if block > 0:
                    part = jnp.where(group == block - 1, high, part)
                parts.append(part)
            band_ref[pl.ds(pl.multiple_of((a + i) * LON, LON), LON), i * LON : (i + 1) * LON] = (
                jnp.concatenate(parts, 0).astype(BF16)
            )
            ring = ring_row(mem, a + i)
            east = pl.multiple_of(halo_row(0, ring), 8)
            west = pl.multiple_of(halo_row(1, ring), 8)
            narrow[pl.ds(east, 8), i * LON : (i + 1) * LON] = jnp.where(group == 15, high, zero)
            narrow[pl.ds(west, 8), i * LON : (i + 1) * LON] = jnp.where(group == 0, low, zero)

    rim_ref[...] = narrow[...].astype(BF16)


def bands(wide):
    return call(
        bands_kernel,
        (shape(MAIN, ROWS * LON, dtype=BF16), shape(HALO, ROWS * LON, dtype=BF16)),
        [VMEM((HALO, ROWS * LON), F32)],
        wide,
    )


def split(value):
    high = value.astype(BF16)
    return high, (value - high.astype(F32)).astype(BF16)


def gathered_rows(wide, start, stride):
    parts = [wide[pl.ds(g * PART + start, GROUP, stride=stride), :] for g in range(4)]
    return jnp.concatenate(parts, 0)


def halo_cells(wide, side, pitch=PART):
    parts = []
    for g in range(4):
        at = (g + 1) * pitch - 48 + side * GROUP
        parts.append(wide[at : at + GROUP])
    return jnp.concatenate(parts, 0)


def halo_field(edges, side, which):
    at = side * EDGES + GROUP + which
    return edges[at : at + 1]


def lat_kernel(x_ref, fields, edges, out_ref, halos, rows):
    mem = lax.axis_index("mem")
    upper = mem < 2
    first = jnp.where(upper, RIM, 0)
    for m in range(0, MEMBERS, 2):
        at = (m // GROUP) * PART + (m % GROUP) * CLAT
        pair = x_ref[at : at + 2 * CLAT].astype(F32)
        one = jnp.where(upper, pair[RIM:CLAT], pair[0:RIM])
        two = jnp.where(upper, pair[CLAT + RIM :], pair[CLAT : CLAT + RIM])
        out_ref[m * RIM : m * RIM + CLAT] = jnp.concatenate([one, two], 0).astype(BF16)
    for g in range(4):
        halos[g * 48 : g * 48 + 48] = x_ref[g * PART + CELLS : (g + 1) * PART].astype(F32)
    lane = lanes((MEMBERS + 8, LON))
    pad = jnp.zeros((7, LON), F32)
    sides = []
    for side in range(2):
        cells = [halo_cells(halos, side, 48), halo_field(edges, side, 0), pad]
        sides.append(jnp.concatenate(cells, 0))
    half = LON // 2
    low = jnp.where(lane < half, sides[0], pltpu.roll(sides[1], half, 1))
    high = jnp.where(lane < half, pltpu.roll(sides[0], half, 1), sides[1])
    both = jnp.where(mem < 2, high, low)
    rows[0:MEMBERS] = both[:MEMBERS]
    rows[MEMBERS : MEMBERS + RIM] = fields[pl.ds(pl.multiple_of(first, 8), RIM), :]
    rows[MEMBERS + RIM :] = both[MEMBERS:]
    out_ref[MEMBERS * RIM :] = rows[...].astype(BF16)


def lat_message(gathered, fields, edges):
    return call(
        lat_kernel,
        shape(LATROWS, LON, dtype=BF16),
        [VMEM((4 * 48, LON), F32), VMEM((LATROWS - MEMBERS * RIM, LON), F32)],
        gathered,
        fields,
        edges,
    )


def rim_steps(mem):
    first = jnp.where(mem < 2, 0, jnp.where(mem == 2, 4, 3))
    return first, jnp.where((mem == 0) | (mem == 3), 2, 1)


def block_steps(mem):
    first = jnp.where(mem == 0, 2, jnp.where(mem == 1, 1, 0))
    return first, jnp.where((mem == 0) | (mem == 3), 3, 4)


def pushes(scaled, corner, band_ref, step):
    at = pl.ds(pl.multiple_of(step * STEP * LON, LON), STEP * LON)
    both = lax.dot_general(
        scaled[:, : ROWS * LON],
        band_ref[at, :],
        (((1,), (1,)), ((), ())),
        preferred_element_type=F32,
    )
    both = both + lax.dot_general(
        scaled[:, ROWS * LON :],
        corner[at, :],
        (((1,), (1,)), ((), ())),
        preferred_element_type=F32,
    )
    return both[:MEMBERS] + both[MEMBERS:]


def by_core(mem, members):
    even = jnp.concatenate([members[0:GROUP], members[2 * GROUP : 3 * GROUP]], 0)
    odd = jnp.concatenate([members[GROUP : 2 * GROUP], members[3 * GROUP :]], 0)
    first = mem % 2 == 0
    return jnp.where(first, even, odd), jnp.where(first, odd, even)


def scale_down(ref, rows):
    values = ref[0:rows]
    largest = jnp.full((16, LON), jnp.max(jnp.abs(values)), F32)
    power = jnp.clip(jnp.round(jnp.log2(largest)) - 8.0, -120.0, 100.0)
    ref[0:rows] = values * jnp.exp2(-power)[0:1]
    ref[rows : rows + 16] = power


def rim_push_kernel(x_ref, fields, edges, band_ref, rim_ref, scaled, corner, wide):
    mem = lax.axis_index("mem")
    wide[...] = x_ref[...].astype(F32)
    for i in range(ROWS):
        own = gathered_rows(wide, ROWS * mem + i, CLAT) * fields[pl.ds(CLAT + ROWS * mem + i, 1), :]
        high, low = split(own)
        scaled[0:MEMBERS, i * LON : (i + 1) * LON] = high
        scaled[MEMBERS:, i * LON : (i + 1) * LON] = low
    lane = lanes((MEMBERS, LON))
    east = halo_cells(wide, 0) * halo_field(edges, 0, 1)
    west = halo_cells(wide, 1) * halo_field(edges, 1, 1)
    east = pltpu.roll(east, (LON - 32 * mem) % LON, 1)
    west = pltpu.roll(west, (LON + 32 - 32 * mem) % LON, 1)
    high, low = split(jnp.where(lane < 32, east, jnp.where(lane < 64, west, 0.0)))
    scaled[0:MEMBERS, ROWS * LON :] = high
    scaled[MEMBERS:, ROWS * LON :] = low
    lane = lanes((8, LON))
    corner[...] = jnp.zeros(corner.shape, BF16)
    tiles = []
    for side in range(2):
        packed = edges[side * EDGES + TAPE : (side + 1) * EDGES]
        tiles.append(
            [
                pltpu.roll(
                    packed[8 * (a // 4) : 8 * (a // 4) + 8],
                    (LON + 32 * side - 32 * (a % 4)) % LON,
                    1,
                )
                for a in range(SPAN)
            ]
        )
    zero = jnp.zeros((8, LON), F32)
    for j in range(WIN):
        edge = []
        for side in range(2):
            tile = zero
            for i in range(ROWS):
                if 0 <= j - i < SPAN:
                    tile = jnp.where(lane // RIM == 4 * side + i, tiles[side][j - i], tile)
            edge.append(tile)
        corner[j * LON : j * LON + 16] = jnp.concatenate([edge[1], zero], 0).astype(BF16)
        corner[j * LON + 112 : j * LON + 128] = jnp.concatenate([zero, edge[0]], 0).astype(BF16)
    zeros = jnp.zeros((MEMBERS, LON), F32)

    @pl.when((mem == 1) | (mem == 2))
    def _():
        first = jnp.where(mem == 1, 0, ROWS)
        for k in range(ROWS):
            rim_ref[pl.ds(first + k, MEMBERS, stride=RIM), :] = zeros

    first, steps = rim_steps(mem)

    @pl.loop(first, first + steps)
    def _(step):
        total = pushes(scaled, corner, band_ref, step)
        for k in range(STEP):
            row = pl.ds(ring_row(mem, step * STEP + k) - CLAT, MEMBERS, stride=RIM)
            rim_ref[row, :] = total[:, k * LON : (k + 1) * LON]

    scale_down(rim_ref, BACK)


def block_push_kernel(scaled, corner, band_ref, out_ref):
    mem = lax.axis_index("mem")
    zeros = jnp.zeros((MEMBERS, LON), F32)

    @pl.when((mem == 0) | (mem == 3))
    def _():
        first = jnp.where(mem == 0, CLAT - ROWS, 0)
        for k in range(ROWS):
            out_ref[pl.ds(first + k, MEMBERS, stride=CLAT), :] = zeros

    first, steps = block_steps(mem)

    @pl.loop(first, first + steps)
    def _(step):
        total = pushes(scaled, corner, band_ref, step)
        for k in range(STEP):
            row = ring_row(mem, step * STEP + k)
            out_ref[pl.ds(row, MEMBERS, stride=CLAT), :] = total[:, k * LON : (k + 1) * LON]


STEP = 4


def rim_push(gathered, fields, edges, band):
    return call(
        rim_push_kernel,
        (
            shape(BACK + 16, LON),
            shape(2 * MEMBERS, (ROWS + 1) * LON, dtype=BF16),
            shape(MAIN, LON, dtype=BF16),
            shape(4 * PART, LON),
        ),
        [],
        gathered,
        fields,
        edges,
        band,
        flops=10**6,
    )


def block_push(scaled, corner, band):
    return call(
        block_push_kernel,
        shape(MEMBERS * CLAT, LON),
        [],
        scaled,
        corner,
        band,
        flops=10**6,
    )


def first_kernel(
    wide, lat_ref, fields, edges, band_ref, rim_ref, push_ref,
    keep_ref, send_ref, window, halos,
    wide_lat, scaled,
):
    mem = lax.axis_index("mem")
    wide_lat[...] = lat_ref[...].astype(F32)
    base = MEMBERS * RIM
    pad = jnp.zeros((DEPTH - MEMBERS - 1, LON), F32)
    for j in range(WIN):
        ring = ring_row(mem, j)

        @pl.when(ring < CLAT)
        def _():
            window[j, 0:MEMBERS] = gathered_rows(wide, ring, CLAT)
            window[j, MEMBERS:] = jnp.concatenate([fields[pl.ds(ring, 1), :], pad], 0)

        @pl.when(ring >= CLAT)
        def _():
            window[j, 0:MEMBERS] = wide_lat[pl.ds(ring - CLAT, MEMBERS, stride=RIM), :]
            row = wide_lat[pl.ds(base + MEMBERS + ring - CLAT, 1), :]
            window[j, MEMBERS:] = jnp.concatenate([row, pad], 0)

    for side in range(2):
        halos[side, 0:MEMBERS] = halo_cells(wide, side)
        halos[side, MEMBERS:] = jnp.concatenate([halo_field(edges, side, 0), pad], 0)
    halos[2, 0:MEMBERS] = wide_lat[base : base + MEMBERS]
    last = wide_lat[base + MEMBERS + RIM : base + MEMBERS + RIM + 1]
    halos[2, MEMBERS:] = jnp.concatenate([last, pad], 0)

    def put(at, cells):
        high, low = split(cells[0:MEMBERS] * cells[MEMBERS : MEMBERS + 1])
        scaled[0:MEMBERS, at : at + LON] = high
        scaled[MEMBERS:, at : at + LON] = low

    for j in range(WIN):
        put(j * LON, window[j])
    for k in range(3):
        put(MAIN + k * LON, halos[k])
    both = jnp.dot(scaled[:, :MAIN], band_ref[...], preferred_element_type=F32)
    both = both + jnp.dot(scaled[:, MAIN:], rim_ref[...], preferred_element_type=F32)
    total = both[:MEMBERS] + both[MEMBERS:]
    v_rows = fields[0:CLAT] * SHARE
    core = mem % 2
    for half in range(2):
        for take, target in ((core, keep_ref), (1 - core, send_ref)):
            for m in range(GROUP):
                at = pl.multiple_of((2 * half + take) * CELLS + m * CLAT, 8)
                to = half * CELLS + m * CLAT
                target[to : to + CLAT] = push_ref[pl.ds(at, CLAT), :] * v_rows
    for i in range(ROWS):
        at = pl.ds(ROWS * mem + i, 2 * GROUP, stride=CLAT)
        c_row = fields[pl.ds(CLAT + ROWS * mem + i, 1), :] * SHARE
        keep, send = by_core(mem, total[:, i * LON : (i + 1) * LON] * c_row)
        keep_ref[at, :] = keep_ref[at, :] + keep
        send_ref[at, :] = send_ref[at, :] + send


def first_sum(wide, lat_halo, fields, edges, band, rim, pushed):
    return call(
        first_kernel,
        (
            shape(2 * CELLS, LON),
            shape(2 * CELLS, LON),
            shape(WIN, DEPTH, LON),
            shape(3, DEPTH, LON),
        ),
        [
            VMEM((LATROWS, LON), F32),
            VMEM((2 * MEMBERS, MAIN + HALO), BF16),
        ],
        wide,
        lat_halo,
        fields,
        edges,
        band,
        rim,
        pushed,
        flops=10**6,
    )


def add_back(mem, take, half, at, back_ref, fields, target):
    first = jnp.where(mem < 2, RIM, 0)
    rows = fields[pl.ds(pl.multiple_of(first, 8), RIM), :] * SHARE
    rows = rows * jnp.exp2(back_ref[BACK : BACK + 1])
    start = (2 * half + take) * GROUP * RIM
    for m in range(GROUP):
        source = pl.ds(pl.multiple_of(start + m * RIM, 8), RIM)
        to = pl.ds(pl.multiple_of(at + m * CLAT + first, 8), RIM)
        target[to, :] = target[to, :] + back_ref[source, :] * rows


def near_kernel(part_ref, back_ref, fields, send_ref):
    mem = lax.axis_index("mem")
    send_ref[...] = part_ref[...]
    for half in range(2):
        add_back(mem, 1 - mem % 2, half, half * CELLS, back_ref, fields, send_ref)


def near_parts(part, back, fields):
    return call(near_kernel, shape(2 * CELLS, LON), [], part, back, fields)


def far_kernel(keep_ref, more_ref, back_ref, fields, mine_ref, send_ref):
    mem = lax.axis_index("mem")
    far = mem // 2
    for take, target in ((far, mine_ref), (1 - far, send_ref)):
        at = pl.ds(pl.multiple_of(take * CELLS, 8), CELLS)
        target[0:CELLS] = keep_ref[at, :] + more_ref[at, :]
        add_back(mem, mem % 2, take, 0, back_ref, fields, target)
    scale_down(send_ref, CELLS)


def far_parts(keep, more, back, fields):
    return call(
        far_kernel, (shape(CELLS, LON), shape(CELLS + 16, LON)), [],
        keep, more, back, fields,
    )


def taper_part(window, halos, fields, flat, own, turned, product, shifted, taps_of):
    mem = lax.axis_index("mem")
    used = range(taps_of[0], taps_of[-1] + ROWS)
    for j in used:
        turned[j * LON : (j + 1) * LON, :] = window[j].T.astype(BF16)
    for k in range(3):
        turned[MAIN + k * LON : MAIN + (k + 1) * LON, :] = halos[k].T.astype(BF16)
    keep = rows_of((DEPTH, LON)) < MEMBERS
    for i in range(ROWS):
        own[:, i * LON : (i + 1) * LON] = jnp.where(keep, window[RIM + i], 0.0).astype(BF16)
    own[:, ROWS * LON :] = jnp.where(rows_of((DEPTH, LON)) == MEMBERS, 1.0, 0.0).astype(BF16)
    for j in [*used, WIN, WIN + 1, WIN + 2]:
        at = j * LON
        product[at : at + LON] = jnp.dot(turned[at : at + LON], own[...], preferred_element_type=F32)
    lane = lanes((8, LON))
    wide_lane = lanes((24, LON))

    def diagonals(j, column):
        ring = ring_row(mem, j)
        east = pl.multiple_of(MAIN + halo_row(0, ring), 8)
        west = pl.multiple_of(MAIN + halo_row(1, ring), 8)
        cells = [product[pl.ds(west, 8), column : column + LON]]
        for block in range(CLAT):
            at = pl.multiple_of(j * LON + 8 * block, 8)
            cells.append(product[pl.ds(at, 8), column : column + LON])
        cells.append(product[pl.ds(east, 8), column : column + LON])
        for bit in (8, 4, 2, 1):
            take = (lane & (8 * bit)) != 0
            cells = [jnp.where(take, cells[s + bit], cells[s]) for s in range(len(cells) - bit)]
        taps = jnp.concatenate(cells, 0)
        for bit in (1, 2, 4):
            taps = jnp.where((wide_lane & bit) != 0, pltpu.roll(taps, 24 - bit, 0), taps)
        return taps

    @pl.loop(used[0], used[-1] + 1)
    def _(j):
        shifted[j] = diagonals(j, ROWS * LON)

    @pl.loop(taps_of[0], taps_of[-1] + 1)
    def _(a):
        for i in range(ROWS):
            c_row = fields[pl.ds(CLAT + ROWS * mem + i, 1), :] * SHARE
            taps = diagonals(a + i, i * LON) * shifted[a + i] * c_row
            flat[pl.ds(a * SPAN * ROWS + i, SPAN, stride=ROWS), :] = taps[0:SPAN]


EARLY = 2


def early_kernel(window, halos, fields, flat, *scratch):
    taper_part(window, halos, fields, flat, *scratch, range(EARLY))


def late_kernel(window, halos, fields, early, taper_ref, flat, *scratch):
    taper_part(window, halos, fields, flat, *scratch, range(EARLY, SPAN))
    for tap in range(TAPS):
        source = early if tap < EARLY * SPAN else flat
        taper_ref[tap] = source[tap * ROWS : tap * ROWS + ROWS]


def taper_scratch():
    return [
        VMEM((DEPTH, (ROWS + 1) * LON), BF16),
        VMEM((MAIN + HALO, DEPTH), BF16),
        VMEM((MAIN + HALO, (ROWS + 1) * LON), F32),
        VMEM((WIN, 24, LON), F32),
    ]


def early_taps(window, halos, fields):
    return call(
        early_kernel, shape(EARLY * SPAN * ROWS + 32, LON), taper_scratch(),
        window, halos, fields, limit=24, flops=2 * 10**10,
    )


def late_taps(window, halos, fields, early):
    return call(
        late_kernel, shape(TAPS, ROWS, LON), [VMEM((TAPE_ROWS, LON), F32), *taper_scratch()],
        window, halos, fields, early, limit=24, flops=10**6,
    )


def body(anomalies, vector, cotangent, taper):
    blocks = lax.axis_size("lat")
    strips = lax.axis_size("lon")
    own = jnp.concatenate([anomalies.reshape(CELLS, LON), vector, cotangent], 0)
    first, second, wide, fields = edge_messages(own, taper)
    swaps = ([], [])
    for s in range(strips):
        there = (s + 1) % strips
        swaps[1 - s % 2].extend([(s, there), (there, s)])
    first = lax.ppermute(first, "lon", swaps[0])
    second = lax.ppermute(second, "lon", swaps[1])
    band, rim = bands(wide)
    first, second, band, rim = lax.optimization_barrier((first, second, band, rim))
    message, edges = call(
        message_kernel, (shape(PART, LON, dtype=BF16), shape(2 * EDGES, LON)), [],
        own, first, second,
    )
    gathered = lax.all_gather(message, "mem", axis=0, tiled=True)

    down = [(4 * z + m, 4 * z + 4 + m) for z in range(blocks - 1) for m in (0, 1)]
    up = [(4 * z + 4 + m, 4 * z + m) for z in range(blocks - 1) for m in (2, 3)]
    message = lat_message(gathered, fields, edges)
    message, gathered = lax.optimization_barrier((message, gathered))
    lat_halo = lax.ppermute(message, ("lat", "mem"), down + up)
    pushed_out, scaled, corner, wide = rim_push(gathered, fields, edges, band)
    back = lax.ppermute(
        pushed_out.astype(jnp.float16), ("lat", "mem"), [(b, a) for a, b in down + up]
    )
    pushed = block_push(scaled, corner, band)
    keep, send, window, halos = first_sum(
        wide, lat_halo, fields, edges, band, rim, pushed
    )
    early = early_taps(window, halos, fields)
    back, send, early = lax.optimization_barrier((back, send, early))
    back = back.astype(F32)
    send = near_parts(send, back, fields)
    more = lax.ppermute(send, "mem", [(0, 1), (1, 0), (2, 3), (3, 2)])
    mine, send = far_parts(keep, more, back, fields)
    half = lax.ppermute(send.astype(jnp.float16), "mem", [(0, 2), (2, 0), (1, 3), (3, 1)])
    mine, early = lax.optimization_barrier((mine, early))
    grad_taper = late_taps(window, halos, fields, early)
    more = half.astype(F32)
    grad_anomalies = mine + more[:CELLS] * jnp.exp2(more[CELLS : CELLS + 1])
    grad_anomalies = grad_anomalies.reshape(GROUP, CLAT, LON)
    return grad_taper, grad_anomalies


def solution(mesh):
    placed = (
        P("mem", "lat", "lon"),
        P("lat", "lon"),
        P("lat", "lon"),
        P(None, ("lat", "mem"), "lon"),
    )
    return jax.shard_map(
        body,
        mesh=mesh,
        in_specs=placed,
        out_specs=(P(None, ("lat", "mem"), "lon"), P("mem", "lat", "lon")),
        check_vma=False,
    )
```

```python
import jax
import jax.numpy as jnp
from jax import lax
from jax.experimental import pallas as pl
from jax.experimental.pallas import tpu as pltpu
from jax.sharding import PartitionSpec as P

SPAN = 17
RIM = 8
TAPS = SPAN * SPAN
ROWS = 4
CLAT = 16
LON = 128
WIN = ROWS + 2 * RIM
RING = CLAT + RIM
GROUP = 20
MEMBERS = 80
DEPTH = 88
CELLS = GROUP * CLAT
EDGES = 64
TAPE = 24
PART = CELLS + 48
HALO = 3 * LON
MAIN = WIN * LON
BACK = MEMBERS * RIM
LATROWS = MEMBERS * RIM + MEMBERS + RIM + 8
TAPE_ROWS = 1184
F32 = jnp.float32
BF16 = jnp.bfloat16
VMEM = pltpu.VMEM
SHARE = 1.0 / (MEMBERS - 1)


def lanes(shape):
    return lax.broadcasted_iota(jnp.int32, shape, len(shape) - 1)


def rows_of(shape):
    return lax.broadcasted_iota(jnp.int32, shape, len(shape) - 2)


def shape(*dims, dtype=F32):
    return jax.ShapeDtypeStruct(dims, dtype)


def call(kernel, out_shape, scratch, *args, limit=16, flops=0):
    return pl.pallas_call(
        kernel,
        out_shape=out_shape,
        in_specs=[pl.BlockSpec(memory_space=VMEM)] * len(args),
        out_specs=jax.tree.map(lambda _: pl.BlockSpec(memory_space=VMEM), out_shape),
        scratch_shapes=scratch,
        compiler_params=pltpu.CompilerParams(vmem_limit_bytes=limit * 2**20),
        cost_estimate=pl.CostEstimate(flops=flops, bytes_accessed=2**20, transcendentals=0),
    )(*args)


def edges_kernel(
    own_ref, taper_ref, first_ref, second_ref, wide, fields, cells
):
    for tap in range(TAPS):
        wide[tap * ROWS : tap * ROWS + ROWS] = taper_ref[tap].astype(F32)
    wide[TAPS * ROWS :] = jnp.zeros((TAPE_ROWS - TAPS * ROWS, LON), F32)
    own = own_ref[...].astype(F32)
    fields[...] = own[CELLS:]
    cells[0 : CELLS + 2 * CLAT] = own
    cells[CELLS + 2 * CLAT :] = jnp.zeros((2 * CLAT, LON), F32)
    lane = lanes((TAPE, LON))
    left = jnp.zeros((TAPE, LON), F32)
    right = jnp.zeros((TAPE, LON), F32)
    for lat in range(CLAT):
        part = cells[pl.ds(lat, TAPE, stride=CLAT), :]
        mine = lane // RIM == lat
        left = jnp.where(mine, pltpu.roll(part, RIM * lat, 1), left)
        right = jnp.where(mine, pltpu.roll(part, (RIM * lat + RIM) % LON, 1), right)
    left_rows = [left]
    right_rows = [right]
    lane = lanes((8, LON))
    row = rows_of((8, LON))
    for block in range(5):
        left = jnp.zeros((8, LON), F32)
        right = jnp.zeros((8, LON), F32)
        for sub in range(4):
            a = block * 4 + sub
            if a >= SPAN:
                continue
            for i in range(ROWS):
                to = sub * 32 + i * RIM
                mine = lane // RIM == to // RIM
                part = wide[pl.ds(a * SPAN * ROWS + i, 8, stride=ROWS), :]
                left = jnp.where(mine, pltpu.roll(part, to, 1), left)
                part = wide[pl.ds((a * SPAN + 9) * ROWS + i, 8, stride=ROWS), :]
                right = jnp.where(mine, pltpu.roll(part, (to + RIM) % LON, 1), right)
        for bit in (1, 2, 4):
            moved = pltpu.roll(left, bit, 0)
            moved = jnp.where(row >= bit, moved, 0.0)
            left = jnp.where((lane & bit) != 0, moved, left)
            moved = pltpu.roll(right, 8 - bit, 0)
            moved = jnp.where(row < 8 - bit, moved, 0.0)
            right = jnp.where(((7 - lane) & bit) != 0, moved, right)
        left_rows.append(left)
        right_rows.append(right)
    left = jnp.concatenate(left_rows, 0)
    right = jnp.concatenate(right_rows, 0)
    odd = lax.axis_index("lon") % 2 == 1
    first_ref[...] = jnp.where(odd, right, left).astype(BF16)
    second_ref[...] = jnp.where(odd, left, right).astype(BF16)


def edge_messages(own, taper):
    return call(
        edges_kernel,
        (
            shape(EDGES, LON, dtype=BF16),
            shape(EDGES, LON, dtype=BF16),
            shape(TAPE_ROWS, LON),
            shape(2 * CLAT, LON),
        ),
        [VMEM(((GROUP + 4) * CLAT, LON), F32)],
        own,
        taper,
    )


def message_kernel(own_ref, first_ref, second_ref, out_ref, edges):
    out_ref[0:CELLS] = own_ref[0:CELLS]
    first = first_ref[...].astype(F32)
    second = second_ref[...].astype(F32)
    odd = lax.axis_index("lon") % 2 == 1
    east = jnp.where(odd, first, second)
    west = jnp.where(odd, second, first)
    edges[0:EDGES] = east
    edges[EDGES:] = west
    halos = [east[0:GROUP], west[0:GROUP], jnp.zeros((8, LON), F32)]
    out_ref[CELLS:] = jnp.concatenate(halos, 0).astype(BF16)


def ring_row(mem, j):
    lat = ROWS * mem - RIM + j
    return jnp.where(lat < 0, lat + RING, lat)


def halo_row(side, ring):
    inside = side * LON + RIM * ring
    outside = 2 * LON + side * (LON // 2) + RIM * (ring - CLAT)
    return jnp.where(ring < CLAT, inside, outside)


def bands_kernel(wide, band_ref, rim_ref, narrow):
    mem = lax.axis_index("mem")
    narrow[...] = jnp.zeros(narrow.shape, F32)
    for i in range(ROWS):
        for j in range(WIN):
            if j < i or j > i + SPAN - 1:
                band_ref[j * LON : (j + 1) * LON, i * LON : (i + 1) * LON] = jnp.zeros(
                    (LON, LON), BF16
                )
    lane = lanes((24, LON))
    row = rows_of((24, LON))
    group = lanes((8, LON)) // 8
    zero = jnp.zeros((8, LON), F32)

    @pl.loop(0, SPAN)
    def _(a):
        for i in range(ROWS):
            taps = wide[pl.ds(a * SPAN * ROWS + i, 24, stride=ROWS), :]
            taps = jnp.where(row < SPAN, taps, 0.0)
            for bit in (1, 2, 4):
                taps = jnp.where((lane & bit) != 0, pltpu.roll(taps, bit, 0), taps)
            low, mid, high = taps[0:8], taps[8:16], taps[16:24]
            parts = []
            for block in range(CLAT):
                part = jnp.where(group == block, mid, zero)
                if block < 15:
                    part = jnp.where(group == block + 1, low, part)
                if block > 0:
                    part = jnp.where(group == block - 1, high, part)
                parts.append(part)
            band_ref[pl.ds(pl.multiple_of((a + i) * LON, LON), LON), i * LON : (i + 1) * LON] = (
                jnp.concatenate(parts, 0).astype(BF16)
            )
            ring = ring_row(mem, a + i)
            east = pl.multiple_of(halo_row(0, ring), 8)
            west = pl.multiple_of(halo_row(1, ring), 8)
            narrow[pl.ds(east, 8), i * LON : (i + 1) * LON] = jnp.where(group == 15, high, zero)
            narrow[pl.ds(west, 8), i * LON : (i + 1) * LON] = jnp.where(group == 0, low, zero)

    rim_ref[...] = narrow[...].astype(BF16)


def bands(wide):
    return call(
        bands_kernel,
        (shape(MAIN, ROWS * LON, dtype=BF16), shape(HALO, ROWS * LON, dtype=BF16)),
        [VMEM((HALO, ROWS * LON), F32)],
        wide,
    )


def split(value):
    high = value.astype(BF16)
    return high, (value - high.astype(F32)).astype(BF16)


def gathered_rows(wide, start, stride):
    parts = [wide[pl.ds(g * PART + start, GROUP, stride=stride), :] for g in range(4)]
    return jnp.concatenate(parts, 0)


def halo_cells(wide, side, pitch=PART):
    parts = []
    for g in range(4):
        at = (g + 1) * pitch - 48 + side * GROUP
        parts.append(wide[at : at + GROUP])
    return jnp.concatenate(parts, 0)


def halo_field(edges, side, which):
    at = side * EDGES + GROUP + which
    return edges[at : at + 1]


def lat_kernel(x_ref, fields, edges, out_ref, halos, rows):
    mem = lax.axis_index("mem")
    upper = mem < 2
    first = jnp.where(upper, RIM, 0)
    for m in range(0, MEMBERS, 2):
        at = (m // GROUP) * PART + (m % GROUP) * CLAT
        pair = x_ref[at : at + 2 * CLAT].astype(F32)
        one = jnp.where(upper, pair[RIM:CLAT], pair[0:RIM])
        two = jnp.where(upper, pair[CLAT + RIM :], pair[CLAT : CLAT + RIM])
        out_ref[m * RIM : m * RIM + CLAT] = jnp.concatenate([one, two], 0).astype(BF16)
    for g in range(4):
        halos[g * 48 : g * 48 + 48] = x_ref[g * PART + CELLS : (g + 1) * PART].astype(F32)
    lane = lanes((MEMBERS + 8, LON))
    pad = jnp.zeros((7, LON), F32)
    sides = []
    for side in range(2):
        cells = [halo_cells(halos, side, 48), halo_field(edges, side, 0), pad]
        sides.append(jnp.concatenate(cells, 0))
    half = LON // 2
    low = jnp.where(lane < half, sides[0], pltpu.roll(sides[1], half, 1))
    high = jnp.where(lane < half, pltpu.roll(sides[0], half, 1), sides[1])
    both = jnp.where(mem < 2, high, low)
    rows[0:MEMBERS] = both[:MEMBERS]
    rows[MEMBERS : MEMBERS + RIM] = fields[pl.ds(pl.multiple_of(first, 8), RIM), :]
    rows[MEMBERS + RIM :] = both[MEMBERS:]
    out_ref[MEMBERS * RIM :] = rows[...].astype(BF16)


def lat_message(gathered, fields, edges):
    return call(
        lat_kernel,
        shape(LATROWS, LON, dtype=BF16),
        [VMEM((4 * 48, LON), F32), VMEM((LATROWS - MEMBERS * RIM, LON), F32)],
        gathered,
        fields,
        edges,
    )


def rim_steps(mem):
    first = jnp.where(mem < 2, 0, jnp.where(mem == 2, 4, 3))
    return first, jnp.where((mem == 0) | (mem == 3), 2, 1)


def block_steps(mem):
    first = jnp.where(mem == 0, 2, jnp.where(mem == 1, 1, 0))
    return first, jnp.where((mem == 0) | (mem == 3), 3, 4)


def pushes(scaled, corner, band_ref, step):
    at = pl.ds(pl.multiple_of(step * STEP * LON, LON), STEP * LON)
    both = lax.dot_general(
        scaled[:, : ROWS * LON],
        band_ref[at, :],
        (((1,), (1,)), ((), ())),
        preferred_element_type=F32,
    )
    both = both + lax.dot_general(
        scaled[:, ROWS * LON :],
        corner[at, :],
        (((1,), (1,)), ((), ())),
        preferred_element_type=F32,
    )
    return both[:MEMBERS] + both[MEMBERS:]


def by_core(mem, members):
    even = jnp.concatenate([members[0:GROUP], members[2 * GROUP : 3 * GROUP]], 0)
    odd = jnp.concatenate([members[GROUP : 2 * GROUP], members[3 * GROUP :]], 0)
    first = mem % 2 == 0
    return jnp.where(first, even, odd), jnp.where(first, odd, even)


def scale_down(ref, rows):
    values = ref[0:rows]
    largest = jnp.full((16, LON), jnp.max(jnp.abs(values)), F32)
    power = jnp.clip(jnp.round(jnp.log2(largest)) - 8.0, -120.0, 100.0)
    ref[0:rows] = values * jnp.exp2(-power)[0:1]
    ref[rows : rows + 16] = power


def rim_push_kernel(x_ref, fields, edges, band_ref, rim_ref, scaled, corner, wide):
    mem = lax.axis_index("mem")
    wide[...] = x_ref[...].astype(F32)
    for i in range(ROWS):
        own = gathered_rows(wide, ROWS * mem + i, CLAT) * fields[pl.ds(CLAT + ROWS * mem + i, 1), :]
        high, low = split(own)
        scaled[0:MEMBERS, i * LON : (i + 1) * LON] = high
        scaled[MEMBERS:, i * LON : (i + 1) * LON] = low
    lane = lanes((MEMBERS, LON))
    east = halo_cells(wide, 0) * halo_field(edges, 0, 1)
    west = halo_cells(wide, 1) * halo_field(edges, 1, 1)
    east = pltpu.roll(east, (LON - 32 * mem) % LON, 1)
    west = pltpu.roll(west, (LON + 32 - 32 * mem) % LON, 1)
    high, low = split(jnp.where(lane < 32, east, jnp.where(lane < 64, west, 0.0)))
    scaled[0:MEMBERS, ROWS * LON :] = high
    scaled[MEMBERS:, ROWS * LON :] = low
    lane = lanes((8, LON))
    corner[...] = jnp.zeros(corner.shape, BF16)
    tiles = []
    for side in range(2):
        packed = edges[side * EDGES + TAPE : (side + 1) * EDGES]
        tiles.append(
            [
                pltpu.roll(
                    packed[8 * (a // 4) : 8 * (a // 4) + 8],
                    (LON + 32 * side - 32 * (a % 4)) % LON,
                    1,
                )
                for a in range(SPAN)
            ]
        )
    zero = jnp.zeros((8, LON), F32)
    for j in range(WIN):
        edge = []
        for side in range(2):
            tile = zero
            for i in range(ROWS):
                if 0 <= j - i < SPAN:
                    tile = jnp.where(lane // RIM == 4 * side + i, tiles[side][j - i], tile)
            edge.append(tile)
        corner[j * LON : j * LON + 16] = jnp.concatenate([edge[1], zero], 0).astype(BF16)
        corner[j * LON + 112 : j * LON + 128] = jnp.concatenate([zero, edge[0]], 0).astype(BF16)
    zeros = jnp.zeros((MEMBERS, LON), F32)

    @pl.when((mem == 1) | (mem == 2))
    def _():
        first = jnp.where(mem == 1, 0, ROWS)
        for k in range(ROWS):
            rim_ref[pl.ds(first + k, MEMBERS, stride=RIM), :] = zeros

    first, steps = rim_steps(mem)

    @pl.loop(first, first + steps)
    def _(step):
        total = pushes(scaled, corner, band_ref, step)
        for k in range(STEP):
            row = pl.ds(ring_row(mem, step * STEP + k) - CLAT, MEMBERS, stride=RIM)
            rim_ref[row, :] = total[:, k * LON : (k + 1) * LON]

    scale_down(rim_ref, BACK)


def block_push_kernel(scaled, corner, band_ref, out_ref):
    mem = lax.axis_index("mem")
    zeros = jnp.zeros((MEMBERS, LON), F32)

    @pl.when((mem == 0) | (mem == 3))
    def _():
        first = jnp.where(mem == 0, CLAT - ROWS, 0)
        for k in range(ROWS):
            out_ref[pl.ds(first + k, MEMBERS, stride=CLAT), :] = zeros

    first, steps = block_steps(mem)

    @pl.loop(first, first + steps)
    def _(step):
        total = pushes(scaled, corner, band_ref, step)
        for k in range(STEP):
            row = ring_row(mem, step * STEP + k)
            out_ref[pl.ds(row, MEMBERS, stride=CLAT), :] = total[:, k * LON : (k + 1) * LON]


STEP = 4


def rim_push(gathered, fields, edges, band):
    return call(
        rim_push_kernel,
        (
            shape(BACK + 16, LON),
            shape(2 * MEMBERS, (ROWS + 1) * LON, dtype=BF16),
            shape(MAIN, LON, dtype=BF16),
            shape(4 * PART, LON),
        ),
        [],
        gathered,
        fields,
        edges,
        band,
        flops=10**6,
    )


def block_push(scaled, corner, band):
    return call(
        block_push_kernel,
        shape(MEMBERS * CLAT, LON),
        [],
        scaled,
        corner,
        band,
        flops=10**6,
    )


def first_kernel(
    wide, lat_ref, fields, edges, band_ref, rim_ref, push_ref,
    keep_ref, send_ref, window, halos,
    wide_lat, scaled,
):
    mem = lax.axis_index("mem")
    wide_lat[...] = lat_ref[...].astype(F32)
    base = MEMBERS * RIM
    pad = jnp.zeros((DEPTH - MEMBERS - 1, LON), F32)
    for j in range(WIN):
        ring = ring_row(mem, j)

        @pl.when(ring < CLAT)
        def _():
            window[j, 0:MEMBERS] = gathered_rows(wide, ring, CLAT)
            window[j, MEMBERS:] = jnp.concatenate([fields[pl.ds(ring, 1), :], pad], 0)

        @pl.when(ring >= CLAT)
        def _():
            window[j, 0:MEMBERS] = wide_lat[pl.ds(ring - CLAT, MEMBERS, stride=RIM), :]
            row = wide_lat[pl.ds(base + MEMBERS + ring - CLAT, 1), :]
            window[j, MEMBERS:] = jnp.concatenate([row, pad], 0)

    for side in range(2):
        halos[side, 0:MEMBERS] = halo_cells(wide, side)
        halos[side, MEMBERS:] = jnp.concatenate([halo_field(edges, side, 0), pad], 0)
    halos[2, 0:MEMBERS] = wide_lat[base : base + MEMBERS]
    last = wide_lat[base + MEMBERS + RIM : base + MEMBERS + RIM + 1]
    halos[2, MEMBERS:] = jnp.concatenate([last, pad], 0)

    def put(at, cells):
        high, low = split(cells[0:MEMBERS] * cells[MEMBERS : MEMBERS + 1])
        scaled[0:MEMBERS, at : at + LON] = high
        scaled[MEMBERS:, at : at + LON] = low

    for j in range(WIN):
        put(j * LON, window[j])
    for k in range(3):
        put(MAIN + k * LON, halos[k])
    both = jnp.dot(scaled[:, :MAIN], band_ref[...], preferred_element_type=F32)
    both = both + jnp.dot(scaled[:, MAIN:], rim_ref[...], preferred_element_type=F32)
    total = both[:MEMBERS] + both[MEMBERS:]
    v_rows = fields[0:CLAT] * SHARE
    core = mem % 2
    for half in range(2):
        for take, target in ((core, keep_ref), (1 - core, send_ref)):
            for m in range(GROUP):
                at = pl.multiple_of((2 * half + take) * CELLS + m * CLAT, 8)
                to = half * CELLS + m * CLAT
                target[to : to + CLAT] = push_ref[pl.ds(at, CLAT), :] * v_rows
    for i in range(ROWS):
        at = pl.ds(ROWS * mem + i, 2 * GROUP, stride=CLAT)
        c_row = fields[pl.ds(CLAT + ROWS * mem + i, 1), :] * SHARE
        keep, send = by_core(mem, total[:, i * LON : (i + 1) * LON] * c_row)
        keep_ref[at, :] = keep_ref[at, :] + keep
        send_ref[at, :] = send_ref[at, :] + send


def first_sum(wide, lat_halo, fields, edges, band, rim, pushed):
    return call(
        first_kernel,
        (
            shape(2 * CELLS, LON),
            shape(2 * CELLS, LON),
            shape(WIN, DEPTH, LON),
            shape(3, DEPTH, LON),
        ),
        [
            VMEM((LATROWS, LON), F32),
            VMEM((2 * MEMBERS, MAIN + HALO), BF16),
        ],
        wide,
        lat_halo,
        fields,
        edges,
        band,
        rim,
        pushed,
        flops=10**6,
    )


def add_back(mem, take, half, at, back_ref, fields, target):
    first = jnp.where(mem < 2, RIM, 0)
    rows = fields[pl.ds(pl.multiple_of(first, 8), RIM), :] * SHARE
    rows = rows * jnp.exp2(back_ref[BACK : BACK + 1])
    start = (2 * half + take) * GROUP * RIM
    for m in range(GROUP):
        source = pl.ds(pl.multiple_of(start + m * RIM, 8), RIM)
        to = pl.ds(pl.multiple_of(at + m * CLAT + first, 8), RIM)
        target[to, :] = target[to, :] + back_ref[source, :] * rows


def near_kernel(part_ref, back_ref, fields, send_ref):
    mem = lax.axis_index("mem")
    send_ref[...] = part_ref[...]
    for half in range(2):
        add_back(mem, 1 - mem % 2, half, half * CELLS, back_ref, fields, send_ref)


def near_parts(part, back, fields):
    return call(near_kernel, shape(2 * CELLS, LON), [], part, back, fields)


def far_kernel(keep_ref, more_ref, back_ref, fields, mine_ref, send_ref):
    mem = lax.axis_index("mem")
    far = mem // 2
    for take, target in ((far, mine_ref), (1 - far, send_ref)):
        at = pl.ds(pl.multiple_of(take * CELLS, 8), CELLS)
        target[0:CELLS] = keep_ref[at, :] + more_ref[at, :]
        add_back(mem, mem % 2, take, 0, back_ref, fields, target)
    scale_down(send_ref, CELLS)


def far_parts(keep, more, back, fields):
    return call(
        far_kernel, (shape(CELLS, LON), shape(CELLS + 16, LON)), [],
        keep, more, back, fields,
    )


def taper_part(window, halos, fields, flat, own, turned, product, shifted, taps_of):
    mem = lax.axis_index("mem")
    used = range(taps_of[0], taps_of[-1] + ROWS)
    for j in used:
        turned[j * LON : (j + 1) * LON, :] = window[j].T.astype(BF16)
    for k in range(3):
        turned[MAIN + k * LON : MAIN + (k + 1) * LON, :] = halos[k].T.astype(BF16)
    keep = rows_of((DEPTH, LON)) < MEMBERS
    for i in range(ROWS):
        own[:, i * LON : (i + 1) * LON] = jnp.where(keep, window[RIM + i], 0.0).astype(BF16)
    own[:, ROWS * LON :] = jnp.where(rows_of((DEPTH, LON)) == MEMBERS, 1.0, 0.0).astype(BF16)
    for j in [*used, WIN, WIN + 1, WIN + 2]:
        at = j * LON
        product[at : at + LON] = jnp.dot(turned[at : at + LON], own[...], preferred_element_type=F32)
    lane = lanes((8, LON))
    wide_lane = lanes((24, LON))

    def diagonals(j, column):
        ring = ring_row(mem, j)
        east = pl.multiple_of(MAIN + halo_row(0, ring), 8)
        west = pl.multiple_of(MAIN + halo_row(1, ring), 8)
        cells = [product[pl.ds(west, 8), column : column + LON]]
        for block in range(CLAT):
            at = pl.multiple_of(j * LON + 8 * block, 8)
            cells.append(product[pl.ds(at, 8), column : column + LON])
        cells.append(product[pl.ds(east, 8), column : column + LON])
        for bit in (8, 4, 2, 1):
            take = (lane & (8 * bit)) != 0
            cells = [jnp.where(take, cells[s + bit], cells[s]) for s in range(len(cells) - bit)]
        taps = jnp.concatenate(cells, 0)
        for bit in (1, 2, 4):
            taps = jnp.where((wide_lane & bit) != 0, pltpu.roll(taps, 24 - bit, 0), taps)
        return taps

    @pl.loop(used[0], used[-1] + 1)
    def _(j):
        shifted[j] = diagonals(j, ROWS * LON)

    @pl.loop(taps_of[0], taps_of[-1] + 1)
    def _(a):
        for i in range(ROWS):
            c_row = fields[pl.ds(CLAT + ROWS * mem + i, 1), :] * SHARE
            taps = diagonals(a + i, i * LON) * shifted[a + i] * c_row
            flat[pl.ds(a * SPAN * ROWS + i, SPAN, stride=ROWS), :] = taps[0:SPAN]


EARLY = 4


def early_kernel(window, halos, fields, flat, *scratch):
    taper_part(window, halos, fields, flat, *scratch, range(EARLY))


def late_kernel(window, halos, fields, early, taper_ref, flat, *scratch):
    taper_part(window, halos, fields, flat, *scratch, range(EARLY, SPAN))
    for tap in range(TAPS):
        source = early if tap < EARLY * SPAN else flat
        taper_ref[tap] = source[tap * ROWS : tap * ROWS + ROWS]


def taper_scratch():
    return [
        VMEM((DEPTH, (ROWS + 1) * LON), BF16),
        VMEM((MAIN + HALO, DEPTH), BF16),
        VMEM((MAIN + HALO, (ROWS + 1) * LON), F32),
        VMEM((WIN, 24, LON), F32),
    ]


def early_taps(window, halos, fields):
    return call(
        early_kernel, shape(EARLY * SPAN * ROWS + 32, LON), taper_scratch(),
        window, halos, fields, limit=24, flops=2 * 10**10,
    )


def late_taps(window, halos, fields, early):
    return call(
        late_kernel, shape(TAPS, ROWS, LON), [VMEM((TAPE_ROWS, LON), F32), *taper_scratch()],
        window, halos, fields, early, limit=24, flops=10**6,
    )


def body(anomalies, vector, cotangent, taper):
    blocks = lax.axis_size("lat")
    strips = lax.axis_size("lon")
    own = jnp.concatenate([anomalies.reshape(CELLS, LON), vector, cotangent], 0)
    first, second, wide, fields = edge_messages(own, taper)
    swaps = ([], [])
    for s in range(strips):
        there = (s + 1) % strips
        swaps[1 - s % 2].extend([(s, there), (there, s)])
    first = lax.ppermute(first, "lon", swaps[0])
    second = lax.ppermute(second, "lon", swaps[1])
    band, rim = bands(wide)
    first, second, band, rim = lax.optimization_barrier((first, second, band, rim))
    message, edges = call(
        message_kernel, (shape(PART, LON, dtype=BF16), shape(2 * EDGES, LON)), [],
        own, first, second,
    )
    gathered = lax.all_gather(message, "mem", axis=0, tiled=True)

    down = [(4 * z + m, 4 * z + 4 + m) for z in range(blocks - 1) for m in (0, 1)]
    up = [(4 * z + 4 + m, 4 * z + m) for z in range(blocks - 1) for m in (2, 3)]
    message = lat_message(gathered, fields, edges)
    message, gathered = lax.optimization_barrier((message, gathered))
    lat_halo = lax.ppermute(message, ("lat", "mem"), down + up)
    pushed_out, scaled, corner, wide = rim_push(gathered, fields, edges, band)
    back = lax.ppermute(
        pushed_out.astype(jnp.float16), ("lat", "mem"), [(b, a) for a, b in down + up]
    )
    pushed = block_push(scaled, corner, band)
    keep, send, window, halos = first_sum(
        wide, lat_halo, fields, edges, band, rim, pushed
    )
    early = early_taps(window, halos, fields)
    back, send, early = lax.optimization_barrier((back, send, early))
    back = back.astype(F32)
    send = near_parts(send, back, fields)
    more = lax.ppermute(send, "mem", [(0, 1), (1, 0), (2, 3), (3, 2)])
    mine, send = far_parts(keep, more, back, fields)
    half = lax.ppermute(send.astype(jnp.float16), "mem", [(0, 2), (2, 0), (1, 3), (3, 1)])
    mine, early = lax.optimization_barrier((mine, early))
    grad_taper = late_taps(window, halos, fields, early)
    more = half.astype(F32)
    grad_anomalies = mine + more[:CELLS] * jnp.exp2(more[CELLS : CELLS + 1])
    grad_anomalies = grad_anomalies.reshape(GROUP, CLAT, LON)
    return grad_taper, grad_anomalies


def solution(mesh):
    placed = (
        P("mem", "lat", "lon"),
        P("lat", "lon"),
        P("lat", "lon"),
        P(None, ("lat", "mem"), "lon"),
    )
    return jax.shard_map(
        body,
        mesh=mesh,
        in_specs=placed,
        out_specs=(P(None, ("lat", "mem"), "lon"), P("mem", "lat", "lon")),
        check_vma=False,
    )
```
